512 devices in a mesh: dp: 8 (over z_hi, core), mp: 64 (over y, z_lo, x).
Axes of the slice: x: 4, y: 4, z: 16 (z_hi: 4, z_lo: 4; z = z_hi * 4 + z_lo), core: 2. Of those that a mesh axis runs over, the one named last changes fastest.
Arguments:
- tokens: bfloat16 [65536, 4096], P(('dp', 'mp')), may hold values from -6 to 6
- grad_out: bfloat16 [14336, 65536], P('mp', 'dp'), may hold values from -0.0234375 to 0.0234375
- basis: bfloat16 [4096, 512], P('mp'), may hold values from -0.09375 to 0.09375
- first_in: float32 [14336, 512], P('mp', 'dp'), may hold values from -6 to 6
- second_in: float32 [14336, 512], P('mp', 'dp'), may hold values from 0.005 to 0.05
Outputs:
- update: bfloat16 [14336, 4096], P('mp', 'dp')
- first_moment: float32 [14336, 512], P('mp', 'dp')
- second_moment: float32 [14336, 512], P('mp', 'dp')
The draws below stay inside these ranges and needn't reach their ends.
All inputs are finite; a program needn't handle non-finite values.
Results may differ from the reference program's by a relative error of at most 0.0049.
Values may be sent and summed in bfloat16 or wider, within the bound.
A program may use at most 64 MiB of HBM per device.

```python
import math
import jax
import jax.numpy as jnp

D = 4096
FF = 14336
RANK = 512
STEP = 10
TOK_DEV = 128
TOKENS = 65536
N_DP = 8
N_MP = 64


def steps_of(key, shape, split, least, top_value):
    level, own = 1.0, jax.random.fold_in(key, 6)
    for dim, parts in split:
        heights = jnp.exp(jax.random.uniform(jax.random.fold_in(own, dim), (parts,), jnp.float32, least / len(split), top_value / len(split)))
        level = level * jnp.repeat(heights, shape[dim] // parts).reshape([-1 if axis == dim else 1 for axis in range(len(shape))])
    return level


def gaussian(own_key, extent, scale, bound, shards=(), dtype=jnp.bfloat16):
    result = jax.random.normal(own_key, extent, jnp.float32) * scale
    if len(shards) > 0:
        result = steps_of(own_key, extent, shards, -0.22, 0.18) * result
    return jnp.clip(result, min=-bound, max=bound).astype(dtype)


def setup_inputs(seed: int = 0) -> dict:
    arg_keys = jax.random.split(jax.random.key(seed), 6)
    return {
        "tokens": gaussian(arg_keys[0], (TOKENS, D), 1.0, 6.0, ((0, 512),)),
        "grad_out": gaussian(arg_keys[1], (FF, TOKENS), ((TOK_DEV * N_DP * N_MP) ** -0.5), 0.0234375, ((0, 64), (1, 8))),
        "basis": gaussian(arg_keys[2], (D, RANK), D ** -0.5, 0.09375, ((0, 64),)),
        "first_in": gaussian(arg_keys[3], (FF, RANK), 1.0, 6.0, ((0, 64), (1, 8)), jnp.float32),
        "second_in": jnp.clip(jnp.exp(math.log(0.05) - 2.3025851 * jax.random.uniform(arg_keys[4], (FF, RANK), jnp.float32) ** steps_of(arg_keys[4], (FF, RANK), ((0, 64), (1, 8)), -0.2, 0.2)), 0.005, 0.05),
    }


beta_one = 0.9
beta_two = 0.999
epsilon = 1e-08

def reference(tokens, grad_out, basis, first_in, second_in):
    projected = jnp.dot(tokens, basis, preferred_element_type=jnp.float32).astype(jnp.bfloat16)
    low_rank = jnp.dot(grad_out, projected, preferred_element_type=jnp.float32)
    first_moment = beta_one * first_in + (1.0 - beta_one) * low_rank
    second_moment = beta_two * second_in + (1.0 - beta_two) * low_rank * low_rank
    corr_one = 1.0 - beta_one ** STEP
    corr_two = 1.0 - beta_two ** STEP
    direction = (first_moment / corr_one / (jnp.sqrt(second_moment / corr_two) + epsilon)).astype(jnp.bfloat16)
    update = jnp.dot(direction, basis.T, preferred_element_type=jnp.float32).astype(jnp.bfloat16)
    return (update, first_moment, second_moment)
```

```python
import jax
import jax.numpy as jnp
from jax import lax
from jax.experimental import pallas as pl
from jax.experimental.pallas import tpu as pltpu
from jax.sharding import PartitionSpec as P

MESH = pl.DeviceIdType.MESH
STEP = 10
beta_one = 0.9
beta_two = 0.999
epsilon = 1e-08

PARTS = 4
ORDERS = {
    0: (("z", "x", "y"), ("x", "y", "z")),
    1: (("z", "y", "x"), ("y", "x", "z")),
}
PROJ = {0: ("x", "y"), 1: ("y", "x")}
SEMS = 192


def low_high(first, second):
    lane = lax.broadcasted_iota(jnp.int32, first.shape, 1)
    low = jnp.where(lane < 64, first, pltpu.roll(second, 64, 1))
    high = jnp.where(lane < 64, pltpu.roll(first, 64, 1), second)
    return low, high


def adam(gradient, first_old, second_old):
    first_new = beta_one * first_old + (1.0 - beta_one) * gradient
    second_new = beta_two * second_old + (1.0 - beta_two) * gradient * gradient
    return first_new, second_new


def main_kernel(
    tok_hbm, grad_hbm, basis_hbm, first_hbm, second_hbm,
    dir_out, low_out, block_out,
    tok, grad, bas, first, second, bbuf, buf, acc, r1_src, r1_dst, own32, pack16, r2_dst, dbuf,
    ssem, rsem, lsem,
):
    dp, mp = lax.axis_index("dp"), lax.axis_index("mp")
    zh, core = dp // 2, dp % 2
    at = {"y": mp // 16, "z": (mp // 4) % 4, "x": mp % 4}

    def device(zh_, core_, y, z, x):
        return (zh_ * 2 + core_, y * 16 + z * 4 + x)

    def ring(dim, step):
        c = dict(at)
        zh_ = zh
        if dim == "z":
            z = (zh * 4 + at["z"] + step + 16) % 16
            zh_, c["z"] = z // 4, z % 4
        else:
            c[dim] = (at[dim] + step + 4) % 4
        return device(zh_, core, c["y"], c["z"], c["x"])

    def cube_z(step):
        return device(zh, core, at["y"], (at["z"] + step) % 4, at["x"])

    def cube(step):
        return device((zh + step) % 4, core, at["y"], at["z"], at["x"])

    sibling = device(zh, 1 - core, at["y"], at["z"], at["x"])

    count = [0]

    def fresh():
        count[0] += 1
        return count[0] - 1

    def remote(src, dst, target, index):
        return pltpu.make_async_remote_copy(
            src_ref=src, dst_ref=dst, send_sem=ssem.at[index], recv_sem=rsem.at[index],
            device_id=target, device_id_type=MESH,
        )

    loads = [
        pltpu.make_async_copy(s, d, lsem.at[i])
        for i, (s, d) in enumerate(
            ((basis_hbm, bas), (tok_hbm, tok), (grad_hbm, grad), (first_hbm, first), (second_hbm, second))
        )
    ]
    for load in loads:
        load.start()

    barrier = pltpu.get_barrier_semaphore()
    partners = [ring("x", 1), ring("x", -1), ring("x", 2), ring("y", 1), ring("y", -1), ring("y", 2)]
    partners += [ring("z", 1), ring("z", -1), ring("z", 2), ring("z", -2)]
    partners += [cube_z(1), cube_z(2), cube_z(3), cube(1), cube(2), cube(3), sibling]
    for partner in partners:
        pl.semaphore_signal(barrier, inc=1, device_id=partner, device_id_type=MESH)

    loads[0].wait()
    for a in range(2):
        t0 = bas[:, a * 256 : a * 256 + 128].astype(jnp.float32)
        t1 = bas[:, a * 256 + 128 : a * 256 + 256].astype(jnp.float32)
        low, high = low_high(t0, t1)
        own = jnp.where(core == 0, low, high).astype(jnp.bfloat16)
        bbuf[2 * a + core, at["y"], at["z"], at["x"]] = own
    pl.semaphore_wait(barrier, len(partners))

    def region(full, **other):
        return tuple(
            slice(None) if d in full else other.get(d, at[d]) for d in ("y", "z", "x")
        )

    bsem = {
        (a, r, k): fresh() for a in range(2) for r in range(2) for k in range(9)
    }
    csem = {(a, r, k): fresh() for a in range(2) for r in range(2) for k in range(4)}
    STEPS = (1, -1, 2)

    def on_cores(body):
        for c in range(2):
            pl.when(core == c)(lambda c=c: body(c))

    def basis_ref(a, c, r, idx):
        return bbuf.at[(2 * a + c, *idx, pl.ds(32 * r, 32))]

    def basis_copy(a, c, r, phase, j):
        order = ORDERS[c][r]
        ref = basis_ref(a, c, r, region(order[:phase]))
        return remote(ref, ref, ring(order[phase], STEPS[j]), bsem[a, r, phase * 3 + j])

    def sibling_copy(a, c, r, k):
        order = ORDERS[c][r]
        last = order[2]
        shift = (0, *STEPS)[k]
        ref = basis_ref(a, c, r, region(order[:2], **{last: (at[last] - shift + 4) % 4}))
        return remote(ref, ref, sibling, csem[a, r, k])

    def basis_start(a, phase):
        def body(c):
            for r in range(2):
                if phase:
                    for j in range(3):
                        basis_copy(a, c, r, phase - 1, j).wait_recv()
                for j in range(3):
                    basis_copy(a, c, r, phase, j).start()
                if phase == 2:
                    sibling_copy(a, c, r, 0).start()
        on_cores(body)

    def basis_end(a):
        def body(c):
            for r in range(2):
                for j in range(3):
                    basis_copy(a, c, r, 2, j).wait_recv()
                    sibling_copy(a, c, r, j + 1).start()
        on_cores(body)

    def basis_settle(a):
        def body(c):
            for r in range(2):
                for k in range(4):
                    sibling_copy(a, 1 - c, r, k).wait_recv()
        on_cores(body)

    def basis_drain(a):
        def body(c):
            for r in range(2):
                for phase in range(3):
                    for j in range(3):
                        basis_copy(a, c, r, phase, j).wait_send()
                for k in range(4):
                    sibling_copy(a, c, r, k).wait_send()
        on_cores(body)

    s1 = {(s, d): fresh() for s in range(PARTS) for d in (1, 2, 3)}
    s2 = {(s, j): fresh() for s in range(PARTS) for j in range(3)}
    s3 = {(s, k, e): fresh() for s in range(PARTS) for k in range(4) for e in (1, -1)}
    sf = {(s, k): fresh() for s in range(PARTS) for k in range(4)}
    SHIFT = (0, *STEPS)

    def proj_ref(s, idx):
        return buf.at[(s, *idx)]

    def copy1(s, d):
        ref = proj_ref(s, region(""))
        return remote(ref, ref, cube_z(d), s1[s, d])

    def copy2(s, j):
        ref = proj_ref(s, region("z"))
        return remote(ref, ref, ring(PROJ[s % 2][0], STEPS[j]), s2[s, j])

    def copy3(s, k, e):
        d2, d3 = PROJ[s % 2]
        ref = proj_ref(s, region("z", **{d2: (at[d2] - SHIFT[k] + 4) % 4}))
        return remote(ref, ref, ring(d3, e), s3[s, k, e])

    def forward(s, k):
        d2, d3 = PROJ[s % 2]
        e = 1 if k % 2 == 0 else -1
        ref = proj_ref(
            s, region("z", **{d2: (at[d2] - SHIFT[k] + 4) % 4, d3: (at[d3] - e + 4) % 4})
        )
        return remote(ref, ref, ring(d3, e), sf[s, k])

    def project(s):
        got = jnp.dot(
            tok[...], bbuf[s].reshape(4096, 128), preferred_element_type=jnp.float32
        )
        buf[s, at["y"], at["z"], at["x"]] = got.astype(jnp.bfloat16)
        for d in (1, 2, 3):
            copy1(s, d).start()

    def stage2(s):
        for d in (1, 2, 3):
            copy1(s, d).wait_recv()
        for j in range(3):
            copy2(s, j).start()
        for e in (1, -1):
            copy3(s, 0, e).start()

    def stage3(s):
        for j in range(3):
            copy2(s, j).wait_recv()
            for e in (1, -1):
                copy3(s, j + 1, e).start()

    def stage4(s):
        for k in range(4):
            for e in (1, -1):
                copy3(s, k, e).wait_recv()
            forward(s, k).start()

    def stage5(s):
        for k in range(4):
            forward(s, k).wait_recv()

    def multiply(s, shift, new=False):
        d3 = PROJ[s % 2][1]
        place = (at[d3] + shift + 4) % 4
        if d3 == "y":
            left = grad[:, pl.ds(pl.multiple_of(place * 2048, 2048), 2048)]
            right = buf[s, place].reshape(2048, 128)
        else:
            left = jnp.concatenate(
                [
                    grad[:, pl.ds(pl.multiple_of((j * 4 + place) * 128, 128), 128)]
                    for j in range(16)
                ],
                axis=1,
            )
            right = buf[s, :, :, place].reshape(2048, 128)
        got = jnp.dot(left, right, preferred_element_type=jnp.float32)
        if new:
            acc[s] = got
        else:
            acc[s] += got

    q1 = [fresh() for _ in range(2)]
    q2 = {(a, d): fresh() for a in range(2) for d in (1, 2, 3)}
    q3 = {d: fresh() for d in (1, 2, 3)}
    q4 = {d: fresh() for d in range(4)}

    def reduce1_copy(a):
        return remote(r1_src.at[a], r1_dst.at[a], sibling, q1[a])

    def reduce1(a):
        r1_src[a] = acc[2 * a + 1 - core]
        reduce1_copy(a).start()

    def reduce2_copy(a, d):
        return remote(pack16.at[a, (zh + d) % 4 % 2], r2_dst.at[d - 1], cube(d), q2[a, d])

    def to_half(a, d):
        return pl.when((zh + d) % 4 // 2 == a)

    def reduce2(a):
        reduce1_copy(a).wait_recv()
        total = acc[2 * a + core] + r1_dst[a]
        for b, packed in enumerate(low_high(total[:112], total[112:])):
            own32[a, b] = packed
            pack16[a, b] = packed.astype(jnp.bfloat16)
        for d in (2, 1, 3):
            to_half(a, d)(lambda d=d: reduce2_copy(a, d).start())

    def direction_copy(d):
        return remote(dbuf.at[dp], dbuf.at[dp], cube(d), q3[d])

    def pass_copy(d):
        slot = (zh - d + 4) % 4 * 2 + core
        return remote(dbuf.at[slot], dbuf.at[slot], sibling, q4[d])

    def reduce3(a):
        @pl.when(zh // 2 == a)
        def _():
            total = own32[a, zh % 2]
            for d in (1, 3, 2):
                reduce2_copy(a, d).wait_recv()
            for d in (1, 3, 2):
                total += r2_dst[d - 1].astype(jnp.float32)
            low_out[...] = total
            old = [jnp.concatenate([v[:112], v[112:]], axis=1) for v in (first[...], second[...])]
            first_new, second_new = adam(total, *old)
            corr_one = 1.0 - beta_one**STEP
            corr_two = 1.0 - beta_two**STEP
            direction = first_new / corr_one / (jnp.sqrt(second_new / corr_two) + epsilon)
            dbuf[dp] = direction.astype(jnp.bfloat16)
            for d in (2, 1, 3):
                direction_copy(d).start()
            pass_copy(0).start()

    basis_start(0, 0)
    basis_start(1, 0)
    basis_start(0, 1)
    basis_start(1, 1)
    basis_start(0, 2)
    basis_start(1, 2)
    basis_end(0)
    loads[1].wait()
    basis_settle(0)
    project(0)
    project(1)
    basis_end(1)
    stage2(0)
    stage2(1)
    basis_settle(1)
    project(2)
    project(3)
    stage3(0)
    stage3(1)
    stage2(2)
    stage2(3)
    loads[2].wait()
    multiply(0, 0, True)
    multiply(1, 0, True)
    stage4(0)
    stage4(1)
    stage3(2)
    stage3(3)
    multiply(0, 1)
    multiply(1, 1)
    multiply(0, -1)
    multiply(1, -1)
    multiply(2, 0, True)
    multiply(3, 0, True)
    block = bbuf.at[:, dp // 2, pl.ds(dp % 2 * 2, 2)]
    keep = pltpu.make_async_copy(block, block_out, lsem.at[5])
    keep.start()
    stage5(0)
    stage5(1)
    multiply(0, 2)
    multiply(1, 2)
    reduce1(0)
    stage4(2)
    stage4(3)
    reduce2(0)
    multiply(2, 1)
    multiply(3, 1)
    multiply(2, -1)
    multiply(3, -1)
    loads[3].wait()
    loads[4].wait()
    stage5(2)
    stage5(3)
    multiply(2, 2)
    multiply(3, 2)
    reduce1(1)
    reduce3(0)
    reduce2(1)
    reduce3(1)
    for d in (1, 3, 2):
        direction_copy(d).wait_recv()
        pass_copy(d).start()
    for d in (0, 1, 3, 2):
        pass_copy(d).wait_recv()
    for a in range(2):
        for c in range(2):
            pair = [dbuf[(2 * a + b) * 2 + c].astype(jnp.float32) for b in range(2)]
            top, bottom = low_high(*pair)
            columns = slice((2 * a + c) * 128, (2 * a + c + 1) * 128)
            dir_out[:112, columns] = top.astype(jnp.bfloat16)
            dir_out[112:, columns] = bottom.astype(jnp.bfloat16)

    for a in range(2):
        basis_drain(a)
    for s in range(PARTS):
        for d in (1, 2, 3):
            copy1(s, d).wait_send()
        for j in range(3):
            copy2(s, j).wait_send()
        for k in range(4):
            for e in (1, -1):
                copy3(s, k, e).wait_send()
            forward(s, k).wait_send()
    for a in range(2):
        reduce1_copy(a).wait_send()
        for d in (1, 2, 3):
            to_half(a, d)(lambda a=a, d=d: reduce2_copy(a, d).wait_send())
    for d in (1, 2, 3):
        direction_copy(d).wait_send()
    for d in range(4):
        pass_copy(d).wait_send()
    keep.wait()
    assert count[0] <= SEMS


def last_kernel(dir_ref, low_ref, block_ref, first_ref, second_ref, update, first_out, second_out):
    total = jnp.zeros((224, 512), jnp.float32)
    for s in range(PARTS):
        total += lax.dot_general(
            dir_ref[:, s * 128 : (s + 1) * 128],
            block_ref[s].reshape(512, 128),
            (((1,), (1,)), ((), ())),
            preferred_element_type=jnp.float32,
        )
    update[...] = total.astype(jnp.bfloat16)
    low = low_ref[...]
    halves = (low[:, :64], pltpu.roll(low, 64, 1)[:, :64])
    for i, gradient in enumerate(halves):
        rows = slice(112 * i, 112 * (i + 1))
        first_new, second_new = adam(gradient, first_ref[rows], second_ref[rows])
        first_out[rows] = first_new
        second_out[rows] = second_new


def per_device(tokens, grad_out, basis, first_in, second_in):
    vmem = pl.BlockSpec(memory_space=pltpu.VMEM)
    anywhere = pl.BlockSpec(memory_space=pl.ANY)
    bf16, f32 = jnp.bfloat16, jnp.float32
    direction, low, block = pl.pallas_call(
        main_kernel,
        out_shape=(
            jax.ShapeDtypeStruct((224, 512), bf16),
            jax.ShapeDtypeStruct((112, 128), f32),
            jax.ShapeDtypeStruct((4, 2, 4, 64, 128), bf16),
        ),
        in_specs=[anywhere] * 5,
        out_specs=(vmem, vmem, anywhere),
        scratch_shapes=[
            pltpu.VMEM((128, 4096), bf16),
            pltpu.VMEM((224, 8192), bf16),
            pltpu.VMEM((64, 512), bf16),
            pltpu.VMEM((224, 64), f32),
            pltpu.VMEM((224, 64), f32),
            pltpu.VMEM((PARTS, 4, 4, 4, 64, 128), bf16),
            pltpu.VMEM((PARTS, 4, 4, 4, 128, 128), bf16),
            pltpu.VMEM((PARTS, 224, 128), f32),
            pltpu.VMEM((2, 224, 128), f32),
            pltpu.VMEM((2, 224, 128), f32),
            pltpu.VMEM((2, 2, 112, 128), f32),
            pltpu.VMEM((2, 2, 112, 128), bf16),
            pltpu.VMEM((3, 112, 128), bf16),
            pltpu.VMEM((8, 112, 128), bf16),
            pltpu.SemaphoreType.DMA((SEMS,)),
            pltpu.SemaphoreType.DMA((SEMS,)),
            pltpu.SemaphoreType.DMA((6,)),
        ],
        compiler_params=pltpu.CompilerParams(
            collective_id=0, has_side_effects=True, vmem_limit_bytes=48 * 2**20
        ),
        name="gather_reduce",
    )(tokens, grad_out, basis, first_in, second_in)
    return pl.pallas_call(
        last_kernel,
        out_shape=(
            jax.ShapeDtypeStruct((224, 512), bf16),
            jax.ShapeDtypeStruct((224, 64), f32),
            jax.ShapeDtypeStruct((224, 64), f32),
        ),
        in_specs=[vmem] * 5,
        out_specs=(vmem,) * 3,
        name="update_moments",
    )(direction, low, block, first_in, second_in)


def solution(mesh):
    in_specs = (P(("dp", "mp"), None), P("mp", "dp"), P("mp", None), P("mp", "dp"), P("mp", "dp"))
    out_specs = (P("mp", "dp"), P("mp", "dp"), P("mp", "dp"))
    return jax.shard_map(
        per_device, mesh=mesh, in_specs=in_specs, out_specs=out_specs, check_vma=False
    )
```

```python
import jax
import jax.numpy as jnp
from jax import lax
from jax.experimental import pallas as pl
from jax.experimental.pallas import tpu as pltpu
from jax.sharding import PartitionSpec as P

MESH = pl.DeviceIdType.MESH
STEP = 10
beta_one = 0.9
beta_two = 0.999
epsilon = 1e-08

PARTS = 4
STEPS = (1, -1, 2)
SHIFT = (0, 1, -1, 2)
SPLITS = (
    (
        ((0, 32, "zxy"), (32, 16, "zyx"), (48, 16, "xyz")),
        ((0, 32, "zyx"), (32, 16, "zxy"), (48, 16, "yxz")),
    ),
    (((0, 64, "zxy"),), ((0, 64, "zyx"),)),
)
SEMS = 320


def low_high(first, second):
    lane = lax.broadcasted_iota(jnp.int32, first.shape, 1)
    low = jnp.where(lane < 64, first, pltpu.roll(second, 64, 1))
    high = jnp.where(lane < 64, pltpu.roll(first, 64, 1), second)
    return low, high


def main_kernel(
    tok_hbm, grad_hbm, basis_hbm, first_hbm, second_hbm,
    update_out, first_out, second_out,
    tok, grad, bas, first, second, bbuf, buf, turned, acc, r1_dst, own32, pack16, r2_dst, dbuf,
    ssem, rsem, lsem,
):
    dp, mp = lax.axis_index("dp"), lax.axis_index("mp")
    zh, core = dp // 2, dp % 2
    at = {"y": mp // 16, "z": (mp // 4) % 4, "x": mp % 4}

    def device(zh_, core_, y, z, x):
        return (zh_ * 2 + core_, y * 16 + z * 4 + x)

    def ring(dim, step):
        c = dict(at)
        zh_ = zh
        if dim == "z":
            z = (zh * 4 + at["z"] + step + 16) % 16
            zh_, c["z"] = z // 4, z % 4
        else:
            c[dim] = (at[dim] + step + 4) % 4
        return device(zh_, core, c["y"], c["z"], c["x"])

    def cube_z(step):
        return device(zh, core, at["y"], (at["z"] + step) % 4, at["x"])

    def cube(step):
        return device((zh + step) % 4, core, at["y"], at["z"], at["x"])

    sibling = device(zh, 1 - core, at["y"], at["z"], at["x"])

    count = [0]

    def fresh():
        count[0] += 1
        return count[0] - 1

    def remote(src, dst, target, index):
        return pltpu.make_async_remote_copy(
            src_ref=src, dst_ref=dst, send_sem=ssem.at[index], recv_sem=rsem.at[index],
            device_id=target, device_id_type=MESH,
        )

    loads = [
        pltpu.make_async_copy(s, d, lsem.at[i])
        for i, (s, d) in enumerate(
            ((basis_hbm, bas), (tok_hbm, tok), (grad_hbm, grad), (first_hbm, first), (second_hbm, second))
        )
    ]
    for load in loads:
        load.start()

    barrier = pltpu.get_barrier_semaphore()
    partners = [ring("x", 1), ring("x", -1), ring("x", 2), ring("y", 1), ring("y", -1), ring("y", 2)]
    partners += [ring("z", 1), ring("z", -1), ring("z", 2), ring("z", -2)]
    partners += [cube_z(1), cube_z(2), cube_z(3), cube(1), cube(2), cube(3), sibling]
    for partner in partners:
        pl.semaphore_signal(barrier, inc=1, device_id=partner, device_id_type=MESH)

    loads[0].wait()
    for a in range(2):
        t0 = bas[:, a * 256 : a * 256 + 128].astype(jnp.float32)
        t1 = bas[:, a * 256 + 128 : a * 256 + 256].astype(jnp.float32)
        low, high = low_high(t0, t1)
        own = jnp.where(core == 0, low, high).astype(jnp.bfloat16)
        bbuf[2 * a + core, at["y"], at["z"], at["x"]] = own
    pl.semaphore_wait(barrier, len(partners))

    def on_cores(body):
        for c in range(2):
            pl.when(core == c)(lambda c=c: body(c))

    def basis_ref(a, c, r, full, **other):
        row, rows, _ = SPLITS[a][c][r]
        idx = tuple(slice(None) if d in full else other.get(d, at[d]) for d in ("y", "z", "x"))
        return bbuf.at[(2 * a + c, *idx, pl.ds(row, rows))]

    def back(dim, k):
        return (at[dim] - SHIFT[k] + 4) % 4

    splits = {a: range(len(SPLITS[a][0])) for a in range(2)}
    b1 = {(a, r, j): fresh() for a in range(2) for r in splits[a] for j in range(3)}
    b2 = {(a, r, j): fresh() for a in range(2) for r in splits[a] for j in range(3)}
    b3 = {(a, r, k, j): fresh() for a in range(2) for r in splits[a] for k in range(4) for j in range(3)}
    bs = {(a, r, k): fresh() for a in range(2) for r in splits[a] for k in range(4)}

    def basis1(a, c, r, j):
        ref = basis_ref(a, c, r, "")
        return remote(ref, ref, ring(SPLITS[a][c][r][2][0], STEPS[j]), b1[a, r, j])

    def basis2(a, c, r, j):
        order = SPLITS[a][c][r][2]
        ref = basis_ref(a, c, r, order[0])
        return remote(ref, ref, ring(order[1], STEPS[j]), b2[a, r, j])

    def basis3(a, c, r, k, j):
        order = SPLITS[a][c][r][2]
        ref = basis_ref(a, c, r, order[0], **{order[1]: back(order[1], k)})
        return remote(ref, ref, ring(order[2], STEPS[j]), b3[a, r, k, j])

    def exchange(a, c, r, k):
        order = SPLITS[a][c][r][2]
        ref = basis_ref(a, c, r, order[:2], **{order[2]: back(order[2], k)})
        return remote(ref, ref, sibling, bs[a, r, k])

    def basis_first(a):
        def body(c):
            for r in splits[a]:
                for j in range(3):
                    basis1(a, c, r, j).start()
        on_cores(body)

    def basis_second(a):
        def body(c):
            for r in splits[a]:
                for j in range(3):
                    basis1(a, c, r, j).wait_recv()
                for j in range(3):
                    basis2(a, c, r, j).start()
                for j in range(3):
                    basis3(a, c, r, 0, j).start()
        on_cores(body)

    def basis_third(a):
        def body(c):
            for j in range(3):
                for r in splits[a]:
                    basis2(a, c, r, j).wait_recv()
                    for j_ in range(3):
                        basis3(a, c, r, j + 1, j_).start()
            for r in splits[a]:
                exchange(a, c, r, 0).start()
        on_cores(body)

    def basis_end(a):
        def body(c):
            for j in range(3):
                for r in splits[a]:
                    for k in range(4):
                        basis3(a, c, r, k, j).wait_recv()
                    exchange(a, c, r, j + 1).start()
        on_cores(body)

    def basis_settle(a):
        def body(c):
            for r in splits[a]:
                for k in range(4):
                    exchange(a, 1 - c, r, k).wait_recv()
        on_cores(body)

    def basis_drain(a):
        def body(c):
            for r in splits[a]:
                for j in range(3):
                    basis1(a, c, r, j).wait_send()
                    basis2(a, c, r, j).wait_send()
                    for k in range(4):
                        basis3(a, c, r, k, j).wait_send()
                for k in range(4):
                    exchange(a, c, r, k).wait_send()
        on_cores(body)

    def flip(i):
        return (core + i) % 2

    def part(i):
        return 2 * (i // 2) + flip(i)

    def line(i, o2=0, o3=0, z=slice(None)):
        f = flip(i)
        y = (at["y"] + f * o2 + (1 - f) * o3 + 4) % 4
        x = (at["x"] + (1 - f) * o2 + f * o3 + 4) % 4
        return buf.at[part(i), y, z, x]

    def step2(i, e):
        f = flip(i)
        return device(zh, core, (at["y"] + f * e + 4) % 4, at["z"], (at["x"] + (1 - f) * e + 4) % 4)

    def step3(i, e):
        return step2(i + 1, e)

    FINE = 2
    s1 = {(i, d): fresh() for i in range(PARTS) for d in (1, 2, 3)}
    s2 = {(i, d, e): fresh() for i in range(PARTS) for d in range(4 if i < FINE else 1) for e in (1, -1)}
    f2 = {(i, e): fresh() for i in range(PARTS) for e in (1, -1)}
    s3 = {
        (i, k, d, e): fresh()
        for i in range(PARTS)
        for k in range(4)
        for d in range(4 if i < FINE and k == 0 else 1)
        for e in (1, -1)
    }
    f3 = {(i, k): fresh() for i in range(PARTS) for k in range(4)}

    def z_back(i, d):
        return (at["z"] - d + 4) % 4 if i < FINE else slice(None)

    def copy1(i, d):
        ref = line(i, z=at["z"])
        return remote(ref, ref, cube_z(d), s1[i, d])

    def copy2(i, d, e):
        ref = line(i, z=z_back(i, d))
        return remote(ref, ref, step2(i, e), s2[i, d, e])

    def half2(i, e):
        ref = line(i, o2=-e, z=pl.ds(0 if e == 1 else 2, 2))
        return remote(ref, ref, step2(i, e), f2[i, e])

    def copy3(i, k, d, e):
        ref = line(i, o2=-SHIFT[k], z=z_back(i, d) if k == 0 else slice(None))
        return remote(ref, ref, step3(i, e), s3[i, k, d, e])

    def half3(i, k):
        e = 1 if k % 2 == 0 else -1
        ref = line(i, o2=-SHIFT[k], o3=-e)
        return remote(ref, ref, step3(i, e), f3[i, k])

    def spread(i, d):
        for e in (1, -1):
            copy2(i, d, e).start()
        for e in (1, -1):
            copy3(i, 0, d, e).start()

    def project(i):
        got = jnp.dot(
            tok[...], bbuf[part(i)].reshape(4096, 128), preferred_element_type=jnp.float32
        )
        buf[part(i), at["y"], at["z"], at["x"]] = got.astype(jnp.bfloat16)
        for d in (1, 3, 2):
            copy1(i, d).start()
        if i < FINE:
            spread(i, 0)

    def stage2(i):
        for d in (1, 3, 2):
            copy1(i, d).wait_recv()
            if i < FINE:
                spread(i, d)
        if i >= FINE:
            spread(i, 0)

    def stage3(i):
        for k, e in ((1, 1), (2, -1)):
            for d in range(4 if i < FINE else 1):
                copy2(i, d, e).wait_recv()
            half2(i, e).start()
            for e3 in (1, -1):
                copy3(i, k, 0, e3).start()

    def stage3b(i):
        for e in (1, -1):
            half2(i, e).wait_recv()
        for e3 in (1, -1):
            copy3(i, 3, 0, e3).start()

    def stage4(i):
        for k in range(4):
            for e in (1, -1):
                for d in range(4 if i < FINE and k == 0 else 1):
                    copy3(i, k, d, e).wait_recv()
            half3(i, k).start()

    def stage5(i):
        for k in range(4):
            half3(i, k).wait_recv()

    def gather_drain(i):
        for d in (1, 2, 3):
            copy1(i, d).wait_send()
        for e in (1, -1):
            half2(i, e).wait_send()
            for d in range(4 if i < FINE else 1):
                copy2(i, d, e).wait_send()
                copy3(i, 0, d, e).wait_send()
            for k in range(1, 4):
                copy3(i, k, 0, e).wait_send()
        for k in range(4):
            half3(i, k).wait_send()

    def multiply(i, shift, new=False):
        def body(f):
            place = (at["x" if f else "y"] + shift + 4) % 4
            if f == 0:
                left = grad[:, pl.ds(pl.multiple_of(place * 2048, 2048), 2048)]
                right = buf[part(i), place].reshape(2048, 128)
            else:
                left = jnp.concatenate(
                    [
                        grad[:, pl.ds(pl.multiple_of((j * 4 + place) * 128, 128), 128)]
                        for j in range(16)
                    ],
                    axis=1,
                )
                right = buf[part(i), :, :, place].reshape(2048, 128)
            got = jnp.dot(left, right, preferred_element_type=jnp.float32)
            if new:
                acc[i] = got
            else:
                acc[i] += got

        for f in range(2):
            pl.when(flip(i) == f)(lambda f=f: body(f))

    q1 = [fresh() for _ in range(2)]
    q2 = {(a, d): fresh() for a in range(2) for d in (1, 2, 3)}
    q3 = {d: fresh() for d in (1, 2, 3)}
    q4 = {d: fresh() for d in range(4)}

    def owner(step, a, body):
        pl.when((zh + step + 4) % 4 // 2 == a)(body)

    def reduce1(a):
        return remote(acc.at[2 * a + 1], r1_dst.at[a], sibling, q1[a])

    def reduce2_copy(a, d):
        return remote(pack16.at[a, (zh + d) % 4 % 2], r2_dst.at[d - 1], cube(d), q2[a, d])

    def reduce2(a):
        reduce1(a).wait_recv()
        total = (acc[2 * a] + r1_dst[a]).T
        for b in range(2):
            own32[a, b] = total[b * 64 : (b + 1) * 64]
            pack16[a, b] = total[b * 64 : (b + 1) * 64].astype(jnp.bfloat16)
        for d in (2, 1, 3):
            owner(d, a, lambda d=d: reduce2_copy(a, d).start())

    def slot(zh_, core_):
        return zh_ // 2 * 4 + core_ * 2 + zh_ % 2

    def direction_copy(d):
        ref = dbuf.at[slot(zh, core)]
        return remote(ref, ref, cube(d), q3[d])

    def pass_copy(d):
        ref = dbuf.at[slot((zh - d + 4) % 4, core)]
        return remote(ref, ref, sibling, q4[d])

    def reduce3(a):
        def body():
            total = own32[a, zh % 2]
            for d in (1, 3, 2):
                reduce2_copy(a, d).wait_recv()
            for d in (1, 3, 2):
                total += r2_dst[d - 1].astype(jnp.float32)
            first_new = beta_one * first[...] + (1.0 - beta_one) * total
            second_new = beta_two * second[...] + (1.0 - beta_two) * total * total
            corr_one = 1.0 - beta_one**STEP
            corr_two = 1.0 - beta_two**STEP
            direction = first_new / corr_one / (jnp.sqrt(second_new / corr_two) + epsilon)
            dbuf[slot(zh, core)] = direction.astype(jnp.bfloat16)
            for d in (2, 1, 3):
                direction_copy(d).start()
            pass_copy(0).start()
            first_out[...] = first_new
            second_out[...] = second_new

        owner(0, a, body)

    def pass_on(a):
        for d in (1, 3, 2):
            def body(d=d):
                direction_copy(d).wait_recv()
                pass_copy(d).start()
            owner(-d, a, body)

    def back_project(a):
        for d in (0, 1, 3, 2):
            owner(-d, a, lambda d=d: pass_copy(d).wait_recv())
        total = jnp.zeros((224, 512), jnp.float32)
        for s in (2 * a, 2 * a + 1):
            columns = jnp.concatenate([dbuf[2 * s], dbuf[2 * s + 1]], axis=0)
            columns = columns.astype(jnp.float32).T.astype(jnp.bfloat16)
            total += jnp.dot(columns, turned[s], preferred_element_type=jnp.float32)
        return total

    basis_first(0)
    basis_first(1)
    basis_second(0)
    basis_third(0)
    basis_second(1)
    basis_end(0)
    loads[1].wait()
    project(0)
    basis_third(1)
    basis_settle(0)
    project(1)
    stage2(0)
    stage2(1)
    stage3(0)
    stage3(1)
    basis_end(1)
    project(2)
    basis_settle(1)
    project(3)
    stage3b(0)
    stage3b(1)
    stage2(2)
    stage2(3)
    loads[2].wait()
    multiply(0, 0, True)
    multiply(1, 0, True)
    stage4(0)
    stage4(1)
    stage3(2)
    stage3(3)
    stage3b(2)
    stage3b(3)
    multiply(1, 1)
    multiply(1, -1)
    multiply(0, 1)
    multiply(0, -1)
    for s in range(PARTS):
        block = bbuf[s, dp // 2, pl.ds(dp % 2 * 2, 2)].reshape(512, 128)
        turned[s] = block.astype(jnp.float32).T.astype(jnp.bfloat16)
    stage5(1)
    multiply(1, 2)
    reduce1(0).start()
    stage5(0)
    multiply(0, 2)
    reduce2(0)
    multiply(2, 0, True)
    multiply(3, 0, True)
    stage4(2)
    stage4(3)
    loads[3].wait()
    loads[4].wait()
    multiply(3, 1)
    multiply(3, -1)
    multiply(2, 1)
    multiply(2, -1)
    reduce3(0)
    stage5(3)
    multiply(3, 2)
    reduce1(1).start()
    stage5(2)
    multiply(2, 2)
    reduce2(1)
    pass_on(0)
    total = back_project(0)
    reduce3(1)
    pass_on(1)
    update_out[...] = (total + back_project(1)).astype(jnp.bfloat16)

    for a in range(2):
        basis_drain(a)
    for i in range(PARTS):
        gather_drain(i)
    for a in range(2):
        reduce1(a).wait_send()
        for d in (1, 2, 3):
            owner(d, a, lambda a=a, d=d: reduce2_copy(a, d).wait_send())
    for d in (1, 2, 3):
        direction_copy(d).wait_send()
    for d in range(4):
        pass_copy(d).wait_send()
    assert count[0] <= SEMS


def last_kernel(update_in, first_in, second_in, update, first, second, sems):
    copies = [
        pltpu.make_async_copy(s, d, sems.at[i])
        for i, (s, d) in enumerate(((update_in, update), (first_in, first), (second_in, second)))
    ]
    for copy in copies:
        copy.start()
    for copy in copies:
        copy.wait()


def per_device(tokens, grad_out, basis, first_in, second_in):
    vmem = pl.BlockSpec(memory_space=pltpu.VMEM)
    hbm = pl.BlockSpec(memory_space=pltpu.HBM)
    bf16, f32 = jnp.bfloat16, jnp.float32
    results = pl.pallas_call(
        main_kernel,
        out_shape=(
            pltpu.VMEM((224, 512), bf16),
            pltpu.VMEM((64, 224), f32),
            pltpu.VMEM((64, 224), f32),
        ),
        in_specs=[hbm] * 5,
        out_specs=(vmem,) * 3,
        scratch_shapes=[
            pltpu.VMEM((128, 4096), bf16),
            pltpu.VMEM((224, 8192), bf16),
            pltpu.VMEM((64, 512), bf16),
            pltpu.VMEM((64, 224), f32),
            pltpu.VMEM((64, 224), f32),
            pltpu.VMEM((PARTS, 4, 4, 4, 64, 128), bf16),
            pltpu.VMEM((PARTS, 4, 4, 4, 128, 128), bf16),
            pltpu.VMEM((PARTS, 128, 512), bf16),
            pltpu.VMEM((PARTS, 224, 128), f32),
            pltpu.VMEM((2, 224, 128), f32),
            pltpu.VMEM((2, 2, 64, 224), f32),
            pltpu.VMEM((2, 2, 64, 224), bf16),
            pltpu.VMEM((3, 64, 224), bf16),
            pltpu.VMEM((8, 64, 224), bf16),
            pltpu.SemaphoreType.DMA((SEMS,)),
            pltpu.SemaphoreType.DMA((SEMS,)),
            pltpu.SemaphoreType.DMA((5,)),
        ],
        compiler_params=pltpu.CompilerParams(
            collective_id=0, has_side_effects=True, vmem_limit_bytes=63 * 2**20
        ),
        name="gather_reduce",
    )(tokens, grad_out, basis, first_in.T, second_in.T)
    update, first, second = pl.pallas_call(
        last_kernel,
        out_shape=(
            jax.ShapeDtypeStruct((224, 512), bf16),
            jax.ShapeDtypeStruct((64, 224), f32),
            jax.ShapeDtypeStruct((64, 224), f32),
        ),
        in_specs=[vmem] * 3,
        out_specs=(hbm,) * 3,
        scratch_shapes=[pltpu.SemaphoreType.DMA((3,))],
        name="results",
    )(*results)
    return update, first.T, second.T


def solution(mesh):
    in_specs = (P(("dp", "mp"), None), P("mp", "dp"), P("mp", None), P("mp", "dp"), P("mp", "dp"))
    out_specs = (P("mp", "dp"), P("mp", "dp"), P("mp", "dp"))
    return jax.shard_map(
        per_device, mesh=mesh, in_specs=in_specs, out_specs=out_specs, check_vma=False
    )
```

```python
import jax
import jax.numpy as jnp
from jax import lax
from jax.experimental import pallas as pl
from jax.experimental.pallas import tpu as pltpu
from jax.sharding import PartitionSpec as P

MESH = pl.DeviceIdType.MESH
STEP = 10
beta_one = 0.9
beta_two = 0.999
epsilon = 1e-08

PARTS = 4
STEPS = (1, -1, 2)
SHIFT = (0, 1, -1, 2)
SPLITS = (
    (
        ((0, 32, "zxy"), (32, 16, "zyx"), (48, 16, "xyz")),
        ((0, 32, "zyx"), (32, 16, "zxy"), (48, 16, "yxz")),
    ),
    (
        ((0, 32, "zxy"), (32, 16, "zyx"), (48, 16, "xyz")),
        ((0, 32, "zyx"), (32, 16, "zxy"), (48, 16, "yxz")),
    ),
)
SENDS = 48
RECEIVES = 96


def low_high(first, second):
    lane = lax.broadcasted_iota(jnp.int32, first.shape, 1)
    low = jnp.where(lane < 64, first, pltpu.roll(second, 64, 1))
    high = jnp.where(lane < 64, pltpu.roll(first, 64, 1), second)
    return low, high


def main_kernel(
    tok_hbm, grad_hbm, basis_hbm, first_hbm, second_hbm,
    update_out, first_out, second_out,
    tok, grad, bas, first, second, bbuf, buf, staged, moments, turned, acc, r1_dst, own32, pack16, r2_dst, dbuf,
    ssem, rsem, lsem, hello,
):
    dp, mp = lax.axis_index("dp"), lax.axis_index("mp")
    zh, core = dp // 2, dp % 2
    at = {"y": mp // 16, "z": (mp // 4) % 4, "x": mp % 4}

    def device(zh_, core_, y, z, x):
        return (zh_ * 2 + core_, y * 16 + z * 4 + x)

    def ring(dim, step):
        c = dict(at)
        zh_ = zh
        if dim == "z":
            z = (zh * 4 + at["z"] + step + 16) % 16
            zh_, c["z"] = z // 4, z % 4
        else:
            c[dim] = (at[dim] + step + 4) % 4
        return device(zh_, core, c["y"], c["z"], c["x"])

    def cube_z(step):
        return device(zh, core, at["y"], (at["z"] + step) % 4, at["x"])

    def cube(step):
        return device((zh + step) % 4, core, at["y"], at["z"], at["x"])

    sibling = device(zh, 1 - core, at["y"], at["z"], at["x"])

    sends, receives = {}, {}

    def remote(src, dst, target, out, into):
        return pltpu.make_async_remote_copy(
            src_ref=src, dst_ref=dst,
            send_sem=ssem.at[sends.setdefault(out, len(sends))],
            recv_sem=rsem.at[receives.setdefault(into, len(receives))],
            device_id=target, device_id_type=MESH,
        )

    def sent(ref, out):
        remote(ref, ref, sibling, out, next(iter(receives))).wait_send()

    def received(ref, into):
        remote(ref, ref, sibling, next(iter(sends)), into).wait_recv()

    loads = [
        pltpu.make_async_copy(s, d, lsem.at[i])
        for i, (s, d) in enumerate(
            ((basis_hbm, bas), (tok_hbm, tok.at[core]), (grad_hbm, grad), (first_hbm, first), (second_hbm, second))
        )
    ]
    for load in loads:
        load.start()
    for i in range(PARTS):
        acc[i, 224:] = jnp.zeros((32, 128), jnp.float32)

    barrier = pltpu.get_barrier_semaphore()
    partners = [ring("x", 1), ring("x", -1), ring("x", 2), ring("y", 1), ring("y", -1), ring("y", 2)]
    partners += [ring("z", 1), ring("z", -1), ring("z", 2), ring("z", -2), sibling]
    for partner in partners:
        pl.semaphore_signal(barrier, inc=1, device_id=partner, device_id_type=MESH)

    loads[0].wait()
    for a in range(2):
        t0 = bas[:, a * 256 : a * 256 + 128].astype(jnp.float32)
        t1 = bas[:, a * 256 + 128 : a * 256 + 256].astype(jnp.float32)
        low, high = low_high(t0, t1)
        own = jnp.where(core == 0, low, high).astype(jnp.bfloat16)
        bbuf[2 * a + core, at["y"], at["z"], at["x"]] = own
    pl.semaphore_wait(barrier, len(partners))

    def greet(level):
        for step in (2 * level + 2, -2 * level - 2):
            pl.semaphore_signal(hello.at[level], inc=1, device_id=ring("z", step), device_id_type=MESH)

    def greeted(level):
        pl.semaphore_wait(hello.at[level], 2)

    greet(0)

    def tokens_copy():
        return remote(tok.at[core], tok.at[core], sibling, "tokens", "tokens")

    loads[1].wait()
    tokens_copy().start()

    def on_cores(body):
        for c in range(2):
            pl.when(core == c)(lambda c=c: body(c))

    def basis_ref(a, c, r, full, **other):
        row, rows, _ = SPLITS[a][c][r]
        idx = tuple(slice(None) if d in full else other.get(d, at[d]) for d in ("y", "z", "x"))
        return bbuf.at[(2 * a + c, *idx, pl.ds(row, rows))]

    def back(dim, k):
        return (at[dim] - SHIFT[k] + 4) % 4

    def basis1(a, c, r, j):
        ref = basis_ref(a, c, r, "")
        return remote(ref, ref, ring(SPLITS[a][c][r][2][0], STEPS[j]), ("b1", a), ("b1", a, r))

    def basis2(a, c, r, j):
        order = SPLITS[a][c][r][2]
        ref = basis_ref(a, c, r, order[0])
        return remote(ref, ref, ring(order[1], STEPS[j]), ("b2", a), ("b2", a, r, j))

    def basis3(a, c, r, k, j):
        order = SPLITS[a][c][r][2]
        ref = basis_ref(a, c, r, order[0], **{order[1]: back(order[1], k)})
        return remote(ref, ref, ring(order[2], STEPS[j]), ("b3", a), ("b3", a))

    def basis_first(a):
        def body(c):
            for r in range(3):
                for j in range(3):
                    basis1(a, c, r, j).start()
        on_cores(body)

    def basis_second(a):
        def body(c):
            for r in range(3):
                received(bbuf.at[0, 0, 0, pl.ds(0, 3), pl.ds(0, SPLITS[a][c][r][1])], ("b1", a, r))
                for j in range(3):
                    basis2(a, c, r, j).start()
                for j in range(3):
                    basis3(a, c, r, 0, j).start()
        on_cores(body)

    def basis_third(a):
        def body(c):
            for j in range(3):
                for r in range(3):
                    basis2(a, c, r, j).wait_recv()
                    for j_ in range(3):
                        basis3(a, c, r, j + 1, j_).start()
        on_cores(body)

    def basis_end(a):
        received(bbuf.at[0, pl.ds(0, 3)], ("b3", a))

    def basis_drain(a):
        sent(bbuf.at[0, 0, 0, pl.ds(0, 3)], ("b1", a))
        sent(bbuf.at[0, 0, pl.ds(0, 3)], ("b2", a))
        sent(bbuf.at[0, pl.ds(0, 3)], ("b3", a))

    def block_copy(a):
        other = zh * 2 + 1 - core
        ref = bbuf.at[2 * a + core, other // 2, pl.ds(other % 2 * 2, 2)]
        return remote(ref, ref, sibling, ("block", a), ("block", a))

    def flip(i):
        return (core + i) % 2

    def part(i):
        return 2 * (i // 2) + flip(i)

    def line(i, o2=0, o3=0, z=slice(None)):
        f = flip(i)
        y = (at["y"] + f * o2 + (1 - f) * o3 + 4) % 4
        x = (at["x"] + (1 - f) * o2 + f * o3 + 4) % 4
        return buf.at[part(i), y, z, x]

    def step2(i, e):
        f = flip(i)
        return device(zh, core, (at["y"] + f * e + 4) % 4, at["z"], (at["x"] + (1 - f) * e + 4) % 4)

    def step3(i, e):
        return step2(i + 1, e)

    FINE = 2

    def z_back(i, d):
        return (at["z"] - d + 4) % 4 if i < FINE else slice(None)

    def copy1(i, d):
        ref = line(i, z=at["z"])
        return remote(ref, ref, cube_z(d), ("s1", i), ("s1", i, d if i < FINE else 0))

    def copy2(i, d, e):
        ref = line(i, z=z_back(i, d))
        return remote(ref, ref, step2(i, e), ("s2", i), ("s2", i, e))

    def half2(i, e):
        ref = line(i, o2=-e, z=pl.ds(0 if e == 1 else 2, 2))
        return remote(ref, ref, step2(i, e), ("s2", i), ("f2", i))

    def copy3(i, k, d, e):
        ref = line(i, o2=-SHIFT[k], z=z_back(i, d) if k == 0 else slice(None))
        return remote(ref, ref, step3(i, e), ("s3", i), ("s3", i, k))

    def half3(i, k):
        e = 1 if k % 2 == 0 else -1
        ref = line(i, o2=-SHIFT[k], o3=-e)
        return remote(ref, ref, step3(i, e), ("s3", i), ("f3", i))

    def spread(i, d):
        for e in (1, -1):
            copy2(i, d, e).start()
        for e in (1, -1):
            copy3(i, 0, d, e).start()

    def place(i):
        return buf.at[part(i), at["y"], at["z"], at["x"]]

    def result_copy(a):
        return remote(staged.at[a], place(2 * a), sibling, ("result", a), ("result", a))

    def begin(i):
        for d in (1, 3, 2):
            copy1(i, d).start()
        if i < FINE:
            spread(i, 0)

    def project(a):
        got = jnp.dot(
            tok[...].reshape(256, 4096),
            bbuf[2 * a + core].reshape(4096, 128),
            preferred_element_type=jnp.float32,
        )
        got = got.astype(jnp.bfloat16)
        staged[a] = jnp.where(core == 0, got[128:], got[:128])
        result_copy(a).start()
        buf[2 * a + core, at["y"], at["z"], at["x"]] = jnp.where(core == 0, got[:128], got[128:])
        begin(2 * a)

    def adopt(a):
        result_copy(a).wait_recv()
        begin(2 * a + 1)

    def stage2(i):
        if i < FINE:
            for d in (1, 3, 2):
                copy1(i, d).wait_recv()
                spread(i, d)
        else:
            received(buf.at[0, 0, 0, pl.ds(0, 3)], ("s1", i, 0))
            spread(i, 0)

    def stage3(i):
        for k, e in ((1, 1), (2, -1)):
            received(buf.at[0, 0, 0], ("s2", i, e))
            half2(i, e).start()
            for e3 in (1, -1):
                copy3(i, k, 0, e3).start()

    def stage3b(i):
        received(buf.at[0, 0, 0], ("f2", i))
        for e3 in (1, -1):
            copy3(i, 3, 0, e3).start()

    def stage4(i, which=(0, 1, 2, 3)):
        for k in which:
            received(buf.at[0, 0, pl.ds(0, 2)], ("s3", i, k))
            half3(i, k).start()

    def stage5(i):
        received(buf.at[0, 0], ("f3", i))

    def gather_drain(i):
        sent(buf.at[0, 0, 0, pl.ds(0, 3)], ("s1", i))
        sent(buf.at[0, 0, pl.ds(0, 3)], ("s2", i))
        sent(buf.at[0, pl.ds(0, 3)], ("s3", i))

    def multiply(i, shift, new=False):
        def body(f):
            place = (at["x" if f else "y"] + shift + 4) % 4
            if f == 0:
                left = grad[:, pl.ds(pl.multiple_of(place * 2048, 2048), 2048)]
                right = buf[part(i), place].reshape(2048, 128)
            else:
                left = jnp.concatenate(
                    [
                        grad[:, pl.ds(pl.multiple_of((j * 4 + place) * 128, 128), 128)]
                        for j in range(16)
                    ],
                    axis=1,
                )
                right = buf[part(i), :, :, place].reshape(2048, 128)
            got = jnp.dot(left, right, preferred_element_type=jnp.float32)
            if new:
                acc[i, :224] = got
            else:
                acc[i, :224] += got

        for f in range(2):
            pl.when(flip(i) == f)(lambda f=f: body(f))

    def owner(step, a, body):
        pl.when((zh + step + 4) % 4 // 2 == a)(body)

    def reduce1(a):
        return remote(acc.at[2 * a + 1], r1_dst.at[a], sibling, ("q1", a), ("q1", a))

    def reduce2_copy(a, d):
        return remote(pack16.at[a, (zh + d) % 4 % 2], r2_dst.at[d - 1], cube(d), ("q2", a, d), ("q2", a, d))

    def reduce2(a):
        reduce1(a).wait_recv()
        total = (acc[2 * a] + r1_dst[a]).T
        for b in range(2):
            own32[a, b] = total[b * 64 : (b + 1) * 64]
            pack16[a, b] = total[b * 64 : (b + 1) * 64].astype(jnp.bfloat16)
        for d in (2, 1, 3):
            owner(d, a, lambda d=d: reduce2_copy(a, d).start())

    def slot(zh_, core_):
        return zh_ // 2 * 4 + core_ * 2 + zh_ % 2

    def direction_copy(d):
        ref = dbuf.at[slot(zh, core)]
        return remote(ref, ref, cube(d), ("q3", d), ("q3", d))

    def pass_copy(d):
        ref = dbuf.at[slot((zh - d + 4) % 4, core)]
        return remote(ref, ref, sibling, ("q4", d), ("q4", d))

    keep = [
        pltpu.make_async_copy(moments.at[n], out, lsem.at[5 + n])
        for n, out in enumerate((first_out, second_out))
    ]

    def reduce3(a):
        def body():
            total = own32[a, zh % 2][:, :224]
            for d in (1, 3, 2):
                reduce2_copy(a, d).wait_recv()
            for d in (1, 3, 2):
                total += r2_dst[d - 1][:, :224].astype(jnp.float32)
            first_new = beta_one * first[...] + (1.0 - beta_one) * total
            second_new = beta_two * second[...] + (1.0 - beta_two) * total * total
            corr_one = 1.0 - beta_one**STEP
            corr_two = 1.0 - beta_two**STEP
            direction = first_new / corr_one / (jnp.sqrt(second_new / corr_two) + epsilon)
            mine = slot(zh, core)
            dbuf[mine, :, 128:] = jnp.zeros((64, 128), jnp.bfloat16)
            dbuf[mine, :, :224] = direction.astype(jnp.bfloat16)
            for d in (2, 1, 3):
                direction_copy(d).start()
            pass_copy(0).start()
            moments[0] = first_new
            moments[1] = second_new
            for copy in keep:
                copy.start()

        owner(0, a, body)

    def pass_on(a):
        for d in (1, 3, 2):
            def body(d=d):
                direction_copy(d).wait_recv()
                pass_copy(d).start()
            owner(-d, a, body)

    def back_project(a):
        for d in (0, 1, 3, 2):
            owner(-d, a, lambda d=d: pass_copy(d).wait_recv())
        total = jnp.zeros((256, 512), jnp.float32)
        for s in (2 * a, 2 * a + 1):
            columns = jnp.concatenate([dbuf[2 * s], dbuf[2 * s + 1]], axis=0)
            columns = columns.astype(jnp.float32).T.astype(jnp.bfloat16)
            total += jnp.dot(columns, turned[s], preferred_element_type=jnp.float32)
        return total

    basis_first(0)
    basis_first(1)
    basis_second(0)
    basis_third(0)
    basis_second(1)
    greeted(0)
    greet(1)
    tokens_copy().wait_recv()
    basis_end(0)
    project(0)
    basis_third(1)
    adopt(0)
    stage2(0)
    stage2(1)
    basis_end(1)
    project(1)
    adopt(1)
    for a in range(2):
        block_copy(a).start()
    stage3(0)
    stage3(1)
    stage4(0, (0,))
    stage4(1, (0,))
    stage2(2)
    stage2(3)
    stage3b(0)
    stage3b(1)
    stage4(0, (1, 2))
    stage4(1, (1, 2))
    greeted(1)
    loads[2].wait()
    multiply(0, 0, True)
    multiply(1, 0, True)
    stage3(2)
    stage3(3)
    stage4(0, (3,))
    stage4(1, (3,))
    stage3b(2)
    stage3b(3)
    stage4(2, (0,))
    stage4(3, (0,))
    multiply(1, 1)
    multiply(1, -1)
    multiply(0, 1)
    multiply(0, -1)
    stage5(1)
    multiply(1, 2)
    reduce1(0).start()
    stage5(0)
    multiply(0, 2)
    stage4(2, (1,))
    stage4(3, (1,))
    reduce2(0)
    multiply(2, 0, True)
    multiply(3, 0, True)
    stage4(2, (2,))
    stage4(3, (2,))
    for a in range(2):
        block_copy(a).wait_recv()
    for s in range(PARTS):
        block = bbuf[s, dp // 2, pl.ds(dp % 2 * 2, 2)].reshape(512, 128)
        turned[s] = block.astype(jnp.float32).T.astype(jnp.bfloat16)
    loads[3].wait()
    loads[4].wait()
    stage4(2, (3,))
    stage4(3, (3,))
    reduce3(0)
    multiply(3, 1)
    multiply(3, -1)
    multiply(2, 1)
    multiply(2, -1)
    stage5(3)
    multiply(3, 2)
    reduce1(1).start()
    stage5(2)
    multiply(2, 2)
    reduce2(1)
    reduce3(1)
    pass_on(0)
    total = back_project(0)
    pass_on(1)
    update_out[...] = (total + back_project(1))[:224].astype(jnp.bfloat16)

    tokens_copy().wait_send()
    for a in range(2):
        basis_drain(a)
        result_copy(a).wait_send()
        block_copy(a).wait_send()
    for i in range(PARTS):
        gather_drain(i)
    for a in range(2):
        reduce1(a).wait_send()
        for d in (1, 2, 3):
            owner(d, a, lambda a=a, d=d: reduce2_copy(a, d).wait_send())
    for d in (1, 2, 3):
        direction_copy(d).wait_send()
    for d in range(4):
        pass_copy(d).wait_send()
    for copy in keep:
        copy.wait()
    assert len(sends) <= SENDS and len(receives) <= RECEIVES


def last_kernel(update_in, first_in, second_in, update, first, second, *scratch):
    held, sems = scratch[:3], scratch[3]
    ins, outs = (update_in, first_in, second_in), (update, first, second)
    loads = [pltpu.make_async_copy(s, d, sems.at[i]) for i, (s, d) in enumerate(zip(ins, held))]
    stores = [pltpu.make_async_copy(s, d, sems.at[3 + i]) for i, (s, d) in enumerate(zip(held, outs))]
    for load in loads:
        load.start()
    for load, store in zip(loads, stores):
        load.wait()
        store.start()
    for store in stores:
        store.wait()


def per_device(tokens, grad_out, basis, first_in, second_in):
    vmem = pl.BlockSpec(memory_space=pltpu.VMEM)
    hbm = pl.BlockSpec(memory_space=pltpu.HBM)
    bf16, f32 = jnp.bfloat16, jnp.float32
    outs = (
        jax.ShapeDtypeStruct((224, 512), bf16),
        jax.ShapeDtypeStruct((64, 224), f32),
        jax.ShapeDtypeStruct((64, 224), f32),
    )
    results = pl.pallas_call(
        main_kernel,
        out_shape=outs,
        in_specs=[hbm] * 5,
        out_specs=(vmem, hbm, hbm),
        scratch_shapes=[
            pltpu.VMEM((2, 128, 4096), bf16),
            pltpu.VMEM((224, 8192), bf16),
            pltpu.VMEM((64, 512), bf16),
            pltpu.VMEM((64, 224), f32),
            pltpu.VMEM((64, 224), f32),
            pltpu.VMEM((PARTS, 4, 4, 4, 64, 128), bf16),
            pltpu.VMEM((PARTS, 4, 4, 4, 128, 128), bf16),
            pltpu.VMEM((2, 128, 128), bf16),
            pltpu.VMEM((2, 64, 224), f32),
            pltpu.VMEM((PARTS, 128, 512), bf16),
            pltpu.VMEM((PARTS, 256, 128), f32),
            pltpu.VMEM((2, 256, 128), f32),
            pltpu.VMEM((2, 2, 64, 256), f32),
            pltpu.VMEM((2, 2, 64, 256), bf16),
            pltpu.VMEM((3, 64, 256), bf16),
            pltpu.VMEM((8, 64, 256), bf16),
            pltpu.SemaphoreType.DMA((SENDS,)),
            pltpu.SemaphoreType.DMA((RECEIVES,)),
            pltpu.SemaphoreType.DMA((7,)),
            pltpu.SemaphoreType.REGULAR((2,)),
        ],
        compiler_params=pltpu.CompilerParams(
            collective_id=0, has_side_effects=True, vmem_limit_bytes=66_600_000
        ),
        name="gather_reduce",
    )(tokens, grad_out, basis, first_in.T, second_in.T)
    update, first, second = pl.pallas_call(
        last_kernel,
        out_shape=outs,
        in_specs=[hbm] * 3,
        out_specs=(hbm,) * 3,
        scratch_shapes=[pltpu.VMEM(o.shape, o.dtype) for o in outs] + [pltpu.SemaphoreType.DMA((6,))],
        compiler_params=pltpu.CompilerParams(vmem_limit_bytes=66_600_000),
        name="results",
    )(*results)
    return update, first.T, second.T


def solution(mesh):
    in_specs = (P(("dp", "mp"), None), P("mp", "dp"), P("mp", None), P("mp", "dp"), P("mp", "dp"))
    out_specs = (P("mp", "dp"), P("mp", "dp"), P("mp", "dp"))
    return jax.shard_map(
        per_device, mesh=mesh, in_specs=in_specs, out_specs=out_specs, check_vma=False
    )
```

```python
import jax
import jax.numpy as jnp
from jax import lax
from jax.experimental import pallas as pl
from jax.experimental.pallas import tpu as pltpu
from jax.sharding import PartitionSpec as P

MESH = pl.DeviceIdType.MESH
STEP = 10
beta_one = 0.9
beta_two = 0.999
epsilon = 1e-08

PARTS = 4
STEPS = (1, -1, 2)
SHIFT = (0, 1, -1, 2)
SPLITS = (
    (
        ((0, 32, "zxy"), (32, 16, "zyx"), (48, 16, "xyz")),
        ((0, 32, "zyx"), (32, 16, "zxy"), (48, 16, "yxz")),
    ),
    (
        ((0, 32, "zxy"), (32, 16, "zyx"), (48, 16, "xyz")),
        ((0, 32, "zyx"), (32, 16, "zxy"), (48, 16, "yxz")),
    ),
)
ROWS = (112, 112)
SENDS = 50
RECEIVES = 98


def low_high(first, second):
    lane = lax.broadcasted_iota(jnp.int32, first.shape, 1)
    low = jnp.where(lane < 64, first, pltpu.roll(second, 64, 1))
    high = jnp.where(lane < 64, pltpu.roll(first, 64, 1), second)
    return low, high


def main_kernel(
    tok_hbm, grad_hbm, basis_hbm, first_hbm, second_hbm,
    update_out, first_out, second_out,
    tok, grad, bas, first, second, bbuf, buf, staged, moments, turned, acc, r1_dst, own32, pack16, r2_dst, dbuf,
    ssem, rsem, lsem, hello,
):
    dp, mp = lax.axis_index("dp"), lax.axis_index("mp")
    zh, core = dp // 2, dp % 2
    at = {"y": mp // 16, "z": (mp // 4) % 4, "x": mp % 4}

    def device(zh_, core_, y, z, x):
        return (zh_ * 2 + core_, y * 16 + z * 4 + x)

    def ring(dim, step):
        c = dict(at)
        zh_ = zh
        if dim == "z":
            z = (zh * 4 + at["z"] + step + 16) % 16
            zh_, c["z"] = z // 4, z % 4
        else:
            c[dim] = (at[dim] + step + 4) % 4
        return device(zh_, core, c["y"], c["z"], c["x"])

    def cube_z(step):
        return device(zh, core, at["y"], (at["z"] + step) % 4, at["x"])

    def cube(step):
        return device((zh + step) % 4, core, at["y"], at["z"], at["x"])

    sibling = device(zh, 1 - core, at["y"], at["z"], at["x"])

    sends, receives = {}, {}

    def remote(src, dst, target, out, into):
        return pltpu.make_async_remote_copy(
            src_ref=src, dst_ref=dst,
            send_sem=ssem.at[sends.setdefault(out, len(sends))],
            recv_sem=rsem.at[receives.setdefault(into, len(receives))],
            device_id=target, device_id_type=MESH,
        )

    def sent(ref, out):
        remote(ref, ref, sibling, out, next(iter(receives))).wait_send()

    def received(ref, into):
        remote(ref, ref, sibling, next(iter(sends)), into).wait_recv()

    loads = [
        pltpu.make_async_copy(s, d, lsem.at[i])
        for i, (s, d) in enumerate(
            ((basis_hbm, bas), (tok_hbm, tok.at[core]), (grad_hbm, grad), (first_hbm, first), (second_hbm, second))
        )
    ]
    for load in loads:
        load.start()
    for i in range(PARTS):
        acc[i, 224:] = jnp.zeros((32, 128), jnp.float32)

    barrier = pltpu.get_barrier_semaphore()
    partners = [ring("x", 1), ring("x", -1), ring("x", 2), ring("y", 1), ring("y", -1), ring("y", 2)]
    partners += [ring("z", 1), ring("z", -1), ring("z", 2), ring("z", -2), sibling]
    for partner in partners:
        pl.semaphore_signal(barrier, inc=1, device_id=partner, device_id_type=MESH)

    loads[0].wait()
    for a in range(2):
        t0 = bas[:, a * 256 : a * 256 + 128].astype(jnp.float32)
        t1 = bas[:, a * 256 + 128 : a * 256 + 256].astype(jnp.float32)
        low, high = low_high(t0, t1)
        own = jnp.where(core == 0, low, high).astype(jnp.bfloat16)
        bbuf[2 * a + core, at["y"], at["z"], at["x"]] = own
    pl.semaphore_wait(barrier, len(partners))

    def greet(level):
        for step in (2 * level + 2, -2 * level - 2):
            pl.semaphore_signal(hello.at[level], inc=1, device_id=ring("z", step), device_id_type=MESH)

    def greeted(level):
        pl.semaphore_wait(hello.at[level], 2)

    greet(0)

    def tokens_copy():
        return remote(tok.at[core], tok.at[core], sibling, "tokens", "tokens")

    def on_cores(body):
        for c in range(2):
            pl.when(core == c)(lambda c=c: body(c))

    def basis_ref(a, c, r, full, **other):
        row, rows, _ = SPLITS[a][c][r]
        idx = tuple(slice(None) if d in full else other.get(d, at[d]) for d in ("y", "z", "x"))
        return bbuf.at[(2 * a + c, *idx, pl.ds(row, rows))]

    def back(dim, k):
        return (at[dim] - SHIFT[k] + 4) % 4

    def basis1(a, c, r, j):
        ref = basis_ref(a, c, r, "")
        return remote(ref, ref, ring(SPLITS[a][c][r][2][0], STEPS[j]), ("b1", a), ("b1", a, r))

    def basis2(a, c, r, j):
        order = SPLITS[a][c][r][2]
        ref = basis_ref(a, c, r, order[0])
        return remote(ref, ref, ring(order[1], STEPS[j]), ("b2", a), ("b2", a, r, j))

    def basis3(a, c, r, k, j):
        order = SPLITS[a][c][r][2]
        ref = basis_ref(a, c, r, order[0], **{order[1]: back(order[1], k)})
        return remote(ref, ref, ring(order[2], STEPS[j]), ("b3", a), ("b3", a))

    def basis_first(a):
        def body(c):
            for r in range(3):
                for j in range(3):
                    basis1(a, c, r, j).start()
        on_cores(body)

    def basis_second(a):
        def body(c):
            for r in range(3):
                received(bbuf.at[0, 0, 0, pl.ds(0, 3), pl.ds(0, SPLITS[a][c][r][1])], ("b1", a, r))
                for j in range(3):
                    basis2(a, c, r, j).start()
                for j in range(3):
                    basis3(a, c, r, 0, j).start()
        on_cores(body)

    def basis_third(a):
        def body(c):
            for j in range(3):
                for r in range(3):
                    basis2(a, c, r, j).wait_recv()
                    for j_ in range(3):
                        basis3(a, c, r, j + 1, j_).start()
        on_cores(body)

    def basis_end(a):
        received(bbuf.at[0, pl.ds(0, 3)], ("b3", a))

    def basis_drain(a):
        sent(bbuf.at[0, 0, 0, pl.ds(0, 3)], ("b1", a))
        sent(bbuf.at[0, 0, pl.ds(0, 3)], ("b2", a))
        sent(bbuf.at[0, pl.ds(0, 3)], ("b3", a))

    def block_copy(a):
        other = zh * 2 + 1 - core
        ref = bbuf.at[2 * a + core, other // 2, pl.ds(other % 2 * 2, 2)]
        return remote(ref, ref, sibling, ("block", a), ("block", a))

    def flip(i):
        return (core + i) % 2

    def part(i):
        return 2 * (i // 2) + flip(i)

    def rows_of(i):
        return pl.ds(0, ROWS[i // 2])

    def rest_of(i):
        return pl.ds(ROWS[i // 2], 128 - ROWS[i // 2])

    def line(i, o2=0, o3=0, z=slice(None), rows=None):
        f = flip(i)
        y = (at["y"] + f * o2 + (1 - f) * o3 + 4) % 4
        x = (at["x"] + (1 - f) * o2 + f * o3 + 4) % 4
        return buf.at[part(i), y, z, x, rows_of(i) if rows is None else rows]

    def step2(i, e):
        f = flip(i)
        return device(zh, core, (at["y"] + f * e + 4) % 4, at["z"], (at["x"] + (1 - f) * e + 4) % 4)

    def step3(i, e):
        return step2(i + 1, e)

    FINE = 2

    def z_back(i, d):
        return (at["z"] - d + 4) % 4 if i < FINE else slice(None)

    def copy1(i, d):
        ref = line(i, z=at["z"])
        return remote(ref, ref, cube_z(d), ("s1", i), ("s1", i, d if i < FINE else 0))

    def copy2(i, d, e):
        ref = line(i, z=z_back(i, d))
        return remote(ref, ref, step2(i, e), ("s2", i), ("s2", i, e))

    def half2(i, e):
        ref = line(i, o2=-e, z=pl.ds(0 if e == 1 else 2, 2))
        return remote(ref, ref, step2(i, e), ("s2", i), ("f2", i))

    def copy3(i, k, d, e):
        ref = line(i, o2=-SHIFT[k], z=z_back(i, d) if k == 0 else slice(None))
        return remote(ref, ref, step3(i, e), ("s3", i), ("s3", i, k))

    def half3(i, k):
        e = 1 if k % 2 == 0 else -1
        ref = line(i, o2=-SHIFT[k], o3=-e)
        return remote(ref, ref, step3(i, e), ("s3", i), ("f3", i))

    def rest1(i, j):
        ref = line(i, z=at["z"], rows=rest_of(i))
        return remote(ref, ref, step2(i, STEPS[j]), ("p1", i), ("p1", i))

    def rest2(i, k, j):
        ref = line(i, o2=-SHIFT[k], z=at["z"], rows=rest_of(i))
        return remote(ref, ref, step3(i, STEPS[j]), ("p2", i), ("p2", i))

    def rest3(i, d):
        ref = buf.at[part(i), :, at["z"], :, rest_of(i)]
        return remote(ref, ref, cube_z(d), ("p3", i), ("p3", i))

    def rest_second(i):
        for j in range(3):
            rest2(i, 0, j).start()
        received(buf.at[0, 0, 0, pl.ds(0, 3), rest_of(i)], ("p1", i))
        for k in range(1, 4):
            for j in range(3):
                rest2(i, k, j).start()

    def rest_third(i):
        received(buf.at[0, 0, pl.ds(0, 3), :, rest_of(i)], ("p2", i))
        for d in (1, 3, 2):
            rest3(i, d).start()

    def rest_end(i):
        received(buf.at[0, pl.ds(0, 3), :, :, rest_of(i)], ("p3", i))

    def spread(i, d):
        for e in (1, -1):
            copy2(i, d, e).start()
        for e in (1, -1):
            copy3(i, 0, d, e).start()

    def place(i):
        return buf.at[part(i), at["y"], at["z"], at["x"]]

    def result_copy(a):
        return remote(staged.at[a], place(2 * a), sibling, ("result", a), ("result", a))

    def begin(i):
        for d in (1, 3, 2):
            copy1(i, d).start()
        if i < FINE:
            spread(i, 0)
        for j in range(3):
            rest1(i, j).start()

    def project(a):
        got = jnp.dot(
            tok[...].reshape(256, 4096),
            bbuf[2 * a + core].reshape(4096, 128),
            preferred_element_type=jnp.float32,
        )
        got = got.astype(jnp.bfloat16)
        staged[a] = jnp.where(core == 0, got[128:], got[:128])
        result_copy(a).start()
        buf[2 * a + core, at["y"], at["z"], at["x"]] = jnp.where(core == 0, got[:128], got[128:])
        begin(2 * a)

    def adopt(a):
        result_copy(a).wait_recv()
        begin(2 * a + 1)

    def stage2(i):
        if i < FINE:
            for d in (1, 3, 2):
                copy1(i, d).wait_recv()
                spread(i, d)
        else:
            received(buf.at[0, 0, 0, pl.ds(0, 3), rows_of(i)], ("s1", i, 0))
            spread(i, 0)

    def stage3(i):
        for k, e in ((1, 1), (2, -1)):
            received(buf.at[0, 0, 0, :, rows_of(i)], ("s2", i, e))
            half2(i, e).start()
            for e3 in (1, -1):
                copy3(i, k, 0, e3).start()

    def stage3b(i):
        received(buf.at[0, 0, 0, :, rows_of(i)], ("f2", i))
        for e3 in (1, -1):
            copy3(i, 3, 0, e3).start()

    def stage4(i, which=(0, 1, 2, 3)):
        for k in which:
            received(buf.at[0, 0, pl.ds(0, 2), :, rows_of(i)], ("s3", i, k))
            half3(i, k).start()

    def stage5(i):
        received(buf.at[0, 0, :, :, rows_of(i)], ("f3", i))

    def gather_drain(i):
        sent(buf.at[0, 0, 0, pl.ds(0, 3), rows_of(i)], ("s1", i))
        sent(buf.at[0, 0, pl.ds(0, 3), :, rows_of(i)], ("s2", i))
        sent(buf.at[0, pl.ds(0, 3), :, :, rows_of(i)], ("s3", i))
        sent(buf.at[0, 0, 0, pl.ds(0, 3), rest_of(i)], ("p1", i))
        sent(buf.at[0, 0, pl.ds(0, 3), :, rest_of(i)], ("p2", i))
        sent(buf.at[0, pl.ds(0, 3), :, :, rest_of(i)], ("p3", i))

    def multiply(i, shift, new=False):
        def body(f):
            place = (at["x" if f else "y"] + shift + 4) % 4
            if f == 0:
                left = grad[:, pl.ds(pl.multiple_of(place * 2048, 2048), 2048)]
                right = buf[part(i), place].reshape(2048, 128)
            else:
                left = jnp.concatenate(
                    [
                        grad[:, pl.ds(pl.multiple_of((j * 4 + place) * 128, 128), 128)]
                        for j in range(16)
                    ],
                    axis=1,
                )
                right = buf[part(i), :, :, place].reshape(2048, 128)
            got = jnp.dot(left, right, preferred_element_type=jnp.float32)
            if new:
                acc[i, :224] = got
            else:
                acc[i, :224] += got

        for f in range(2):
            pl.when(flip(i) == f)(lambda f=f: body(f))

    def owner(step, a, body):
        pl.when((zh + step + 4) % 4 // 2 == a)(body)

    def reduce1(a):
        return remote(acc.at[2 * a + 1], r1_dst.at[a], sibling, ("q1", a), ("q1", a))

    def reduce2_copy(a, d):
        return remote(pack16.at[a, (zh + d) % 4 % 2], r2_dst.at[d - 1], cube(d), ("q2", a, d), ("q2", a, d))

    def reduce2(a):
        reduce1(a).wait_recv()
        total = (acc[2 * a] + r1_dst[a]).T
        for b in range(2):
            own32[a, b] = total[b * 64 : (b + 1) * 64]
            pack16[a, b] = total[b * 64 : (b + 1) * 64].astype(jnp.bfloat16)
        for d in (2, 1, 3):
            owner(d, a, lambda d=d: reduce2_copy(a, d).start())

    def slot(zh_, core_):
        return zh_ // 2 * 4 + core_ * 2 + zh_ % 2

    def direction_copy(d):
        ref = dbuf.at[slot(zh, core)]
        return remote(ref, ref, cube(d), ("q3", d), ("q3", d))

    def pass_copy(d):
        ref = dbuf.at[slot((zh - d + 4) % 4, core)]
        return remote(ref, ref, sibling, ("q4", d), ("q4", d))

    keep = [
        pltpu.make_async_copy(moments.at[n], out, lsem.at[5 + n])
        for n, out in enumerate((first_out, second_out))
    ]

    def reduce3(a):
        def body():
            total = own32[a, zh % 2][:, :224]
            for d in (1, 3, 2):
                reduce2_copy(a, d).wait_recv()
            for d in (1, 3, 2):
                total += r2_dst[d - 1][:, :224].astype(jnp.float32)
            first_new = beta_one * first[...] + (1.0 - beta_one) * total
            second_new = beta_two * second[...] + (1.0 - beta_two) * total * total
            corr_one = 1.0 - beta_one**STEP
            corr_two = 1.0 - beta_two**STEP
            direction = first_new / corr_one / (jnp.sqrt(second_new / corr_two) + epsilon)
            mine = slot(zh, core)
            dbuf[mine, :, 128:] = jnp.zeros((64, 128), jnp.bfloat16)
            dbuf[mine, :, :224] = direction.astype(jnp.bfloat16)
            for d in (2, 1, 3):
                direction_copy(d).start()
            pass_copy(0).start()
            moments[0] = first_new
            moments[1] = second_new
            for copy in keep:
                copy.start()

        owner(0, a, body)

    def pass_on(a):
        for d in (1, 3, 2):
            def body(d=d):
                direction_copy(d).wait_recv()
                pass_copy(d).start()
            owner(-d, a, body)

    def back_project(a):
        for d in (0, 1, 3, 2):
            owner(-d, a, lambda d=d: pass_copy(d).wait_recv())
        total = jnp.zeros((256, 512), jnp.float32)
        for s in (2 * a, 2 * a + 1):
            columns = jnp.concatenate([dbuf[2 * s], dbuf[2 * s + 1]], axis=0)
            columns = columns.astype(jnp.float32).T.astype(jnp.bfloat16)
            total += jnp.dot(columns, turned[s], preferred_element_type=jnp.float32)
        return total

    basis_first(0)
    basis_first(1)
    loads[1].wait()
    tokens_copy().start()
    basis_second(0)
    basis_third(0)
    basis_second(1)
    greeted(0)
    greet(1)
    tokens_copy().wait_recv()
    basis_end(0)
    project(0)
    basis_third(1)
    adopt(0)
    stage2(0)
    basis_end(1)
    project(1)
    stage2(1)
    rest_second(0)
    rest_second(1)
    adopt(1)
    for a in range(2):
        block_copy(a).start()
    stage3(0)
    stage3(1)
    rest_third(0)
    rest_third(1)
    rest_second(2)
    rest_second(3)
    stage4(0, (0,))
    stage4(1, (0,))
    stage2(2)
    stage2(3)
    stage3b(0)
    stage3b(1)
    rest_third(2)
    rest_third(3)
    stage4(0, (1, 2))
    stage4(1, (1, 2))
    greeted(1)
    loads[2].wait()
    stage3(2)
    stage3(3)
    stage4(2, (0,))
    stage4(3, (0,))
    stage4(0, (3,))
    stage4(1, (3,))
    rest_end(1)
    multiply(1, 0, True)
    multiply(1, 1)
    multiply(1, -1)
    stage3b(2)
    stage3b(3)
    rest_end(0)
    multiply(0, 0, True)
    multiply(0, 1)
    multiply(0, -1)
    stage4(2, (1, 2))
    stage4(3, (1, 2))
    stage5(1)
    multiply(1, 2)
    reduce1(0).start()
    stage5(0)
    multiply(0, 2)
    reduce2(0)
    rest_end(2)
    multiply(2, 0, True)
    stage4(2, (3,))
    stage4(3, (3,))
    rest_end(3)
    multiply(3, 0, True)
    for a in range(2):
        block_copy(a).wait_recv()
    for s in range(PARTS):
        block = bbuf[s, dp // 2, pl.ds(dp % 2 * 2, 2)].reshape(512, 128)
        turned[s] = block.astype(jnp.float32).T.astype(jnp.bfloat16)
    loads[3].wait()
    loads[4].wait()
    multiply(3, 1)
    multiply(3, -1)
    multiply(2, 1)
    multiply(2, -1)
    stage5(3)
    multiply(3, 2)
    reduce1(1).start()
    stage5(2)
    multiply(2, 2)
    reduce2(1)
    reduce3(0)
    reduce3(1)
    pass_on(0)
    total = back_project(0)
    pass_on(1)
    update_out[...] = (total + back_project(1))[:224].astype(jnp.bfloat16)

    tokens_copy().wait_send()
    for a in range(2):
        basis_drain(a)
        result_copy(a).wait_send()
        block_copy(a).wait_send()
    for i in range(PARTS):
        gather_drain(i)
    for a in range(2):
        reduce1(a).wait_send()
        for d in (1, 2, 3):
            owner(d, a, lambda a=a, d=d: reduce2_copy(a, d).wait_send())
    for d in (1, 2, 3):
        direction_copy(d).wait_send()
    for d in range(4):
        pass_copy(d).wait_send()
    for copy in keep:
        copy.wait()
    assert len(sends) <= SENDS and len(receives) <= RECEIVES


def last_kernel(update_in, first_in, second_in, update, first, second, *scratch):
    held, sems = scratch[:3], scratch[3]
    ins, outs = (update_in, first_in, second_in), (update, first, second)
    loads = [pltpu.make_async_copy(s, d, sems.at[i]) for i, (s, d) in enumerate(zip(ins, held))]
    stores = [pltpu.make_async_copy(s, d, sems.at[3 + i]) for i, (s, d) in enumerate(zip(held, outs))]
    for load in loads:
        load.start()
    for load, store in zip(loads, stores):
        load.wait()
        store.start()
    for store in stores:
        store.wait()


def per_device(tokens, grad_out, basis, first_in, second_in):
    vmem = pl.BlockSpec(memory_space=pltpu.VMEM)
    hbm = pl.BlockSpec(memory_space=pltpu.HBM)
    bf16, f32 = jnp.bfloat16, jnp.float32
    outs = (
        jax.ShapeDtypeStruct((224, 512), bf16),
        jax.ShapeDtypeStruct((64, 224), f32),
        jax.ShapeDtypeStruct((64, 224), f32),
    )
    results = pl.pallas_call(
        main_kernel,
        out_shape=outs,
        in_specs=[hbm] * 5,
        out_specs=(vmem, hbm, hbm),
        scratch_shapes=[
            pltpu.VMEM((2, 128, 4096), bf16),
            pltpu.VMEM((224, 8192), bf16),
            pltpu.VMEM((64, 512), bf16),
            pltpu.VMEM((64, 224), f32),
            pltpu.VMEM((64, 224), f32),
            pltpu.VMEM((PARTS, 4, 4, 4, 64, 128), bf16),
            pltpu.VMEM((PARTS, 4, 4, 4, 128, 128), bf16),
            pltpu.VMEM((2, 128, 128), bf16),
            pltpu.VMEM((2, 64, 224), f32),
            pltpu.VMEM((PARTS, 128, 512), bf16),
            pltpu.VMEM((PARTS, 256, 128), f32),
            pltpu.VMEM((2, 256, 128), f32),
            pltpu.VMEM((2, 2, 64, 256), f32),
            pltpu.VMEM((2, 2, 64, 256), bf16),
            pltpu.VMEM((3, 64, 256), bf16),
            pltpu.VMEM((8, 64, 256), bf16),
            pltpu.SemaphoreType.DMA((SENDS,)),
            pltpu.SemaphoreType.DMA((RECEIVES,)),
            pltpu.SemaphoreType.DMA((7,)),
            pltpu.SemaphoreType.REGULAR((2,)),
        ],
        compiler_params=pltpu.CompilerParams(
            collective_id=0, has_side_effects=True, vmem_limit_bytes=66_600_000
        ),
        name="gather_reduce",
    )(tokens, grad_out, basis, first_in.T, second_in.T)
    update, first, second = pl.pallas_call(
        last_kernel,
        out_shape=outs,
        in_specs=[hbm] * 3,
        out_specs=(hbm,) * 3,
        scratch_shapes=[pltpu.VMEM(o.shape, o.dtype) for o in outs] + [pltpu.SemaphoreType.DMA((6,))],
        compiler_params=pltpu.CompilerParams(vmem_limit_bytes=66_600_000),
        name="results",
    )(*results)
    return update, first.T, second.T


def solution(mesh):
    in_specs = (P(("dp", "mp"), None), P("mp", "dp"), P("mp", None), P("mp", "dp"), P("mp", "dp"))
    out_specs = (P("mp", "dp"), P("mp", "dp"), P("mp", "dp"))
    return jax.shard_map(
        per_device, mesh=mesh, in_specs=in_specs, out_specs=out_specs, check_vma=False
    )
```

```python
import jax
import jax.numpy as jnp
from jax import lax
from jax.experimental import pallas as pl
from jax.experimental.pallas import tpu as pltpu
from jax.sharding import PartitionSpec as P

MESH = pl.DeviceIdType.MESH
STEP = 10
beta_one = 0.9
beta_two = 0.999
epsilon = 1e-08

PARTS = 4
STEPS = (1, -1, 2)
SHIFT = (0, 1, -1, 2)
SPLITS = (
    (
        ((0, 32, "zxy"), (32, 16, "zyx"), (48, 16, "xyz")),
        ((0, 32, "zyx"), (32, 16, "zxy"), (48, 16, "yxz")),
    ),
    (
        ((0, 32, "zxy"), (32, 16, "zyx"), (48, 16, "xyz")),
        ((0, 32, "zyx"), (32, 16, "zxy"), (48, 16, "yxz")),
    ),
)
ROWS = (112, 112)
SENDS = 50
RECEIVES = 98


def low_high(first, second):
    lane = lax.broadcasted_iota(jnp.int32, first.shape, 1)
    low = jnp.where(lane < 64, first, pltpu.roll(second, 64, 1))
    high = jnp.where(lane < 64, pltpu.roll(first, 64, 1), second)
    return low, high


def main_kernel(
    tok_hbm, grad_hbm, basis_hbm, first_hbm, second_hbm,
    update_out, first_out, second_out,
    tok, grad, bas, first, second, bbuf, buf, staged, moments, turned, acc, r1_dst, own32, pack16, r2_dst, dbuf,
    ssem, rsem, lsem, hello,
):
    dp, mp = lax.axis_index("dp"), lax.axis_index("mp")
    zh, core = dp // 2, dp % 2
    at = {"y": mp // 16, "z": (mp // 4) % 4, "x": mp % 4}

    def device(zh_, core_, y, z, x):
        return (zh_ * 2 + core_, y * 16 + z * 4 + x)

    def ring(dim, step):
        c = dict(at)
        zh_ = zh
        if dim == "z":
            z = (zh * 4 + at["z"] + step + 16) % 16
            zh_, c["z"] = z // 4, z % 4
        else:
            c[dim] = (at[dim] + step + 4) % 4
        return device(zh_, core, c["y"], c["z"], c["x"])

    def cube_z(step):
        return device(zh, core, at["y"], (at["z"] + step) % 4, at["x"])

    def cube(step):
        return device((zh + step) % 4, core, at["y"], at["z"], at["x"])

    sibling = device(zh, 1 - core, at["y"], at["z"], at["x"])

    sends, receives = {}, {}

    def remote(src, dst, target, out, into):
        return pltpu.make_async_remote_copy(
            src_ref=src, dst_ref=dst,
            send_sem=ssem.at[sends.setdefault(out, len(sends))],
            recv_sem=rsem.at[receives.setdefault(into, len(receives))],
            device_id=target, device_id_type=MESH,
        )

    def sent(ref, out):
        remote(ref, ref, sibling, out, next(iter(receives))).wait_send()

    def received(ref, into):
        remote(ref, ref, sibling, next(iter(sends)), into).wait_recv()

    loads = [
        pltpu.make_async_copy(s, d, lsem.at[i])
        for i, (s, d) in enumerate(
            ((basis_hbm, bas), (tok_hbm, tok.at[core]), (grad_hbm, grad), (first_hbm, first), (second_hbm, second))
        )
    ]
    for load in loads:
        load.start()
    for i in range(PARTS):
        acc[i, 224:] = jnp.zeros((32, 128), jnp.float32)

    barrier = pltpu.get_barrier_semaphore()
    partners = [ring("x", 1), ring("x", -1), ring("x", 2), ring("y", 1), ring("y", -1), ring("y", 2)]
    partners += [ring("z", 1), ring("z", -1), ring("z", 2), ring("z", -2), sibling]
    for partner in partners:
        pl.semaphore_signal(barrier, inc=1, device_id=partner, device_id_type=MESH)

    loads[0].wait()
    for a in range(2):
        t0 = bas[:, a * 256 : a * 256 + 128].astype(jnp.float32)
        t1 = bas[:, a * 256 + 128 : a * 256 + 256].astype(jnp.float32)
        low, high = low_high(t0, t1)
        own = jnp.where(core == 0, low, high).astype(jnp.bfloat16)
        bbuf[2 * a + core, at["y"], at["z"], at["x"]] = own
    pl.semaphore_wait(barrier, len(partners))

    def greet(level):
        for step in (2 * level + 2, -2 * level - 2):
            pl.semaphore_signal(hello.at[level], inc=1, device_id=ring("z", step), device_id_type=MESH)

    def greeted(level):
        pl.semaphore_wait(hello.at[level], 2)

    greet(0)

    def tokens_copy():
        return remote(tok.at[core], tok.at[core], sibling, "tokens", "tokens")

    def on_cores(body):
        for c in range(2):
            pl.when(core == c)(lambda c=c: body(c))

    def basis_ref(a, c, r, full, **other):
        row, rows, _ = SPLITS[a][c][r]
        idx = tuple(slice(None) if d in full else other.get(d, at[d]) for d in ("y", "z", "x"))
        return bbuf.at[(2 * a + c, *idx, pl.ds(row, rows))]

    def back(dim, k):
        return (at[dim] - SHIFT[k] + 4) % 4

    def basis1(a, c, r, j):
        ref = basis_ref(a, c, r, "")
        return remote(ref, ref, ring(SPLITS[a][c][r][2][0], STEPS[j]), ("b1", a), ("b1", a, r))

    def basis2(a, c, r, j):
        order = SPLITS[a][c][r][2]
        ref = basis_ref(a, c, r, order[0])
        return remote(ref, ref, ring(order[1], STEPS[j]), ("b2", a), ("b2", a, r, j))

    def basis3(a, c, r, k, j):
        order = SPLITS[a][c][r][2]
        ref = basis_ref(a, c, r, order[0], **{order[1]: back(order[1], k)})
        return remote(ref, ref, ring(order[2], STEPS[j]), ("b3", a), ("b3", a))

    def basis_first(a):
        def body(c):
            for r in range(3):
                for j in range(3):
                    basis1(a, c, r, j).start()
        on_cores(body)

    def basis_second(a):
        def body(c):
            for r in range(3):
                received(bbuf.at[0, 0, 0, pl.ds(0, 3), pl.ds(0, SPLITS[a][c][r][1])], ("b1", a, r))
                for j in range(3):
                    basis2(a, c, r, j).start()
            for r in range(3):
                for j in range(3):
                    basis3(a, c, r, 0, j).start()
        on_cores(body)

    def basis_third(a):
        def body(c):
            for j in range(3):
                for r in range(3):
                    basis2(a, c, r, j).wait_recv()
                    for j_ in range(3):
                        basis3(a, c, r, j + 1, j_).start()
        on_cores(body)

    def basis_end(a):
        received(bbuf.at[0, pl.ds(0, 3)], ("b3", a))

    def basis_drain(a):
        sent(bbuf.at[0, 0, 0, pl.ds(0, 3)], ("b1", a))
        sent(bbuf.at[0, 0, pl.ds(0, 3)], ("b2", a))
        sent(bbuf.at[0, pl.ds(0, 3)], ("b3", a))

    def block_copy(a):
        other = zh * 2 + 1 - core
        ref = bbuf.at[2 * a + core, other // 2, pl.ds(other % 2 * 2, 2)]
        return remote(ref, ref, sibling, ("block", a), ("block", a))

    def flip(i):
        return (core + i) % 2

    def part(i):
        return 2 * (i // 2) + flip(i)

    def rows_of(i):
        return pl.ds(0, ROWS[i // 2])

    def rest_of(i):
        return pl.ds(ROWS[i // 2], 128 - ROWS[i // 2])

    def line(i, o2=0, o3=0, z=slice(None), rows=None):
        f = flip(i)
        y = (at["y"] + f * o2 + (1 - f) * o3 + 4) % 4
        x = (at["x"] + (1 - f) * o2 + f * o3 + 4) % 4
        return buf.at[part(i), y, z, x, rows_of(i) if rows is None else rows]

    def step2(i, e):
        f = flip(i)
        return device(zh, core, (at["y"] + f * e + 4) % 4, at["z"], (at["x"] + (1 - f) * e + 4) % 4)

    def step3(i, e):
        return step2(i + 1, e)

    FINE = 2

    def z_back(i, d):
        return (at["z"] - d + 4) % 4 if i < FINE else slice(None)

    def copy1(i, d):
        ref = line(i, z=at["z"])
        return remote(ref, ref, cube_z(d), ("s1", i), ("s1", i, d if i < FINE else 0))

    def copy2(i, d, e):
        ref = line(i, z=z_back(i, d))
        return remote(ref, ref, step2(i, e), ("s2", i), ("s2", i, e))

    def half2(i, e):
        ref = line(i, o2=-e, z=pl.ds(0 if e == 1 else 2, 2))
        return remote(ref, ref, step2(i, e), ("s2", i), ("f2", i))

    def copy3(i, k, d, e):
        ref = line(i, o2=-SHIFT[k], z=z_back(i, d) if k == 0 else slice(None))
        return remote(ref, ref, step3(i, e), ("s3", i), ("s3", i, k))

    def half3(i, k):
        e = 1 if k % 2 == 0 else -1
        ref = line(i, o2=-SHIFT[k], o3=-e)
        return remote(ref, ref, step3(i, e), ("s3", i), ("f3", i))

    def rest1(i, j):
        ref = line(i, z=at["z"], rows=rest_of(i))
        return remote(ref, ref, step2(i, STEPS[j]), ("p1", i), ("p1", i))

    def rest2(i, k, j):
        ref = line(i, o2=-SHIFT[k], z=at["z"], rows=rest_of(i))
        return remote(ref, ref, step3(i, STEPS[j]), ("p2", i), ("p2", i))

    def rest3(i, d):
        ref = buf.at[part(i), :, at["z"], :, rest_of(i)]
        return remote(ref, ref, cube_z(d), ("p3", i), ("p3", i))

    def rest_second(i):
        for j in range(3):
            rest2(i, 0, j).start()
        received(buf.at[0, 0, 0, pl.ds(0, 3), rest_of(i)], ("p1", i))
        for k in range(1, 4):
            for j in range(3):
                rest2(i, k, j).start()

    def rest_third(i):
        received(buf.at[0, 0, pl.ds(0, 3), :, rest_of(i)], ("p2", i))
        for d in (1, 3, 2):
            rest3(i, d).start()

    def rest_end(i):
        received(buf.at[0, pl.ds(0, 3), :, :, rest_of(i)], ("p3", i))

    def spread(i, d):
        for e in (1, -1):
            copy2(i, d, e).start()
        for e in (1, -1):
            copy3(i, 0, d, e).start()

    def place(i):
        return buf.at[part(i), at["y"], at["z"], at["x"]]

    def result_copy(a):
        return remote(staged.at[a], place(2 * a), sibling, ("result", a), ("result", a))

    def begin(i):
        for d in (1, 3, 2):
            copy1(i, d).start()
        if i < FINE:
            spread(i, 0)
        for j in range(3):
            rest1(i, j).start()

    def project(a):
        got = jnp.dot(
            tok[...].reshape(256, 4096),
            bbuf[2 * a + core].reshape(4096, 128),
            preferred_element_type=jnp.float32,
        )
        got = got.astype(jnp.bfloat16)
        staged[a] = jnp.where(core == 0, got[128:], got[:128])
        result_copy(a).start()
        buf[2 * a + core, at["y"], at["z"], at["x"]] = jnp.where(core == 0, got[:128], got[128:])
        begin(2 * a)

    def adopt(a):
        result_copy(a).wait_recv()
        begin(2 * a + 1)

    def stage2(i):
        if i < FINE:
            for d in (1, 3, 2):
                copy1(i, d).wait_recv()
                spread(i, d)
        else:
            received(buf.at[0, 0, 0, pl.ds(0, 3), rows_of(i)], ("s1", i, 0))
            spread(i, 0)

    def stage3(i):
        for k, e in ((1, 1), (2, -1)):
            received(buf.at[0, 0, 0, :, rows_of(i)], ("s2", i, e))
            half2(i, e).start()
            for e3 in (1, -1):
                copy3(i, k, 0, e3).start()

    def stage3b(i):
        received(buf.at[0, 0, 0, :, rows_of(i)], ("f2", i))
        for e3 in (1, -1):
            copy3(i, 3, 0, e3).start()

    def stage4(i, which=(0, 1, 2, 3)):
        for k in which:
            received(buf.at[0, 0, pl.ds(0, 2), :, rows_of(i)], ("s3", i, k))
            half3(i, k).start()

    def stage5(i):
        received(buf.at[0, 0, :, :, rows_of(i)], ("f3", i))

    def gather_drain(i):
        sent(buf.at[0, 0, 0, pl.ds(0, 3), rows_of(i)], ("s1", i))
        sent(buf.at[0, 0, pl.ds(0, 3), :, rows_of(i)], ("s2", i))
        sent(buf.at[0, pl.ds(0, 3), :, :, rows_of(i)], ("s3", i))
        sent(buf.at[0, 0, 0, pl.ds(0, 3), rest_of(i)], ("p1", i))
        sent(buf.at[0, 0, pl.ds(0, 3), :, rest_of(i)], ("p2", i))
        sent(buf.at[0, pl.ds(0, 3), :, :, rest_of(i)], ("p3", i))

    def multiply(i, shift, new=False):
        def body(f):
            place = (at["x" if f else "y"] + shift + 4) % 4
            if f == 0:
                left = grad[:, pl.ds(pl.multiple_of(place * 2048, 2048), 2048)]
                right = buf[part(i), place].reshape(2048, 128)
            else:
                left = jnp.concatenate(
                    [
                        grad[:, pl.ds(pl.multiple_of((j * 4 + place) * 128, 128), 128)]
                        for j in range(16)
                    ],
                    axis=1,
                )
                right = buf[part(i), :, :, place].reshape(2048, 128)
            got = jnp.dot(left, right, preferred_element_type=jnp.float32)
            if new:
                acc[i, :224] = got
            else:
                acc[i, :224] += got

        for f in range(2):
            pl.when(flip(i) == f)(lambda f=f: body(f))

    def owner(step, a, body):
        pl.when((zh + step + 4) % 4 // 2 == a)(body)

    def reduce1(a):
        return remote(acc.at[2 * a + 1], r1_dst.at[a], sibling, ("q1", a), ("q1", a))

    def reduce2_copy(a, d):
        return remote(pack16.at[a, (zh + d) % 4 % 2], r2_dst.at[d - 1], cube(d), ("q2", a, d), ("q2", a, d))

    def reduce2(a):
        reduce1(a).wait_recv()
        total = (acc[2 * a] + r1_dst[a]).T
        for b in range(2):
            own32[a, b] = total[b * 64 : (b + 1) * 64]
            pack16[a, b] = total[b * 64 : (b + 1) * 64].astype(jnp.bfloat16)
        for d in (2, 1, 3):
            owner(d, a, lambda d=d: reduce2_copy(a, d).start())

    def slot(zh_, core_):
        return zh_ // 2 * 4 + core_ * 2 + zh_ % 2

    def direction_copy(d):
        ref = dbuf.at[slot(zh, core)]
        return remote(ref, ref, cube(d), ("q3", d), ("q3", d))

    def pass_copy(d):
        ref = dbuf.at[slot((zh - d + 4) % 4, core)]
        return remote(ref, ref, sibling, ("q4", d), ("q4", d))

    keep = [
        pltpu.make_async_copy(moments.at[n], out, lsem.at[5 + n])
        for n, out in enumerate((first_out, second_out))
    ]

    def reduce3(a):
        def body():
            total = own32[a, zh % 2][:, :224]
            for d in (1, 3, 2):
                reduce2_copy(a, d).wait_recv()
            for d in (1, 3, 2):
                total += r2_dst[d - 1][:, :224].astype(jnp.float32)
            first_new = beta_one * first[...] + (1.0 - beta_one) * total
            second_new = beta_two * second[...] + (1.0 - beta_two) * total * total
            corr_one = 1.0 - beta_one**STEP
            corr_two = 1.0 - beta_two**STEP
            direction = first_new / corr_one / (jnp.sqrt(second_new / corr_two) + epsilon)
            mine = slot(zh, core)
            dbuf[mine, :, 128:] = jnp.zeros((64, 128), jnp.bfloat16)
            dbuf[mine, :, :224] = direction.astype(jnp.bfloat16)
            for d in (2, 1, 3):
                direction_copy(d).start()
            pass_copy(0).start()
            moments[0] = first_new
            moments[1] = second_new
            for copy in keep:
                copy.start()

        owner(0, a, body)

    def pass_on(a):
        for d in (1, 3, 2):
            def body(d=d):
                direction_copy(d).wait_recv()
                pass_copy(d).start()
            owner(-d, a, body)

    def back_project(a):
        for d in (0, 1, 3, 2):
            owner(-d, a, lambda d=d: pass_copy(d).wait_recv())
        total = jnp.zeros((256, 512), jnp.float32)
        for s in (2 * a, 2 * a + 1):
            columns = jnp.concatenate([dbuf[2 * s], dbuf[2 * s + 1]], axis=0)
            columns = columns.astype(jnp.float32).T.astype(jnp.bfloat16)
            total += jnp.dot(columns, turned[s], preferred_element_type=jnp.float32)
        return total

    basis_first(0)
    basis_first(1)
    loads[1].wait()
    tokens_copy().start()
    basis_second(0)
    basis_third(0)
    basis_second(1)
    greeted(0)
    greet(1)
    tokens_copy().wait_recv()
    basis_end(0)
    project(0)
    basis_third(1)
    adopt(0)
    stage2(0)
    basis_end(1)
    project(1)
    stage2(1)
    rest_second(0)
    rest_second(1)
    adopt(1)
    for a in range(2):
        block_copy(a).start()
    stage3(0)
    stage3(1)
    rest_third(0)
    rest_third(1)
    rest_second(2)
    rest_second(3)
    stage4(0, (0,))
    stage4(1, (0,))
    stage2(2)
    stage2(3)
    stage3b(0)
    stage3b(1)
    rest_third(2)
    rest_third(3)
    stage4(0, (1, 2))
    stage4(1, (1, 2))
    greeted(1)
    loads[2].wait()
    stage3(2)
    stage3(3)
    stage4(2, (0,))
    stage4(3, (0,))
    stage4(0, (3,))
    stage4(1, (3,))
    rest_end(1)
    multiply(1, 0, True)
    multiply(1, 1)
    multiply(1, -1)
    stage3b(2)
    rest_end(0)
    multiply(0, 0, True)
    multiply(0, 1)
    multiply(0, -1)
    stage3b(3)
    stage4(2, (1, 2))
    stage4(3, (1, 2))
    stage5(1)
    multiply(1, 2)
    reduce1(0).start()
    stage5(0)
    multiply(0, 2)
    reduce2(0)
    rest_end(2)
    multiply(2, 0, True)
    stage4(2, (3,))
    stage4(3, (3,))
    rest_end(3)
    multiply(3, 0, True)
    for a in range(2):
        block_copy(a).wait_recv()
    for s in range(PARTS):
        block = bbuf[s, dp // 2, pl.ds(dp % 2 * 2, 2)].reshape(512, 128)
        turned[s] = block.astype(jnp.float32).T.astype(jnp.bfloat16)
    loads[3].wait()
    loads[4].wait()
    multiply(3, 1)
    multiply(3, -1)
    multiply(2, 1)
    multiply(2, -1)
    stage5(3)
    multiply(3, 2)
    reduce1(1).start()
    stage5(2)
    multiply(2, 2)
    reduce2(1)
    reduce3(0)
    reduce3(1)
    pass_on(0)
    total = back_project(0)
    pass_on(1)
    update_out[...] = (total + back_project(1))[:224].astype(jnp.bfloat16)

    tokens_copy().wait_send()
    for a in range(2):
        basis_drain(a)
        result_copy(a).wait_send()
        block_copy(a).wait_send()
    for i in range(PARTS):
        gather_drain(i)
    for a in range(2):
        reduce1(a).wait_send()
        for d in (1, 2, 3):
            owner(d, a, lambda a=a, d=d: reduce2_copy(a, d).wait_send())
    for d in (1, 2, 3):
        direction_copy(d).wait_send()
    for d in range(4):
        pass_copy(d).wait_send()
    for copy in keep:
        copy.wait()
    assert len(sends) <= SENDS and len(receives) <= RECEIVES


def last_kernel(update_in, first_in, second_in, update, first, second, *scratch):
    held, sems = scratch[:3], scratch[3]
    ins, outs = (update_in, first_in, second_in), (update, first, second)
    loads = [pltpu.make_async_copy(s, d, sems.at[i]) for i, (s, d) in enumerate(zip(ins, held))]
    stores = [pltpu.make_async_copy(s, d, sems.at[3 + i]) for i, (s, d) in enumerate(zip(held, outs))]
    for load in loads:
        load.start()
    for load, store in zip(loads, stores):
        load.wait()
        store.start()
    for store in stores:
        store.wait()


def per_device(tokens, grad_out, basis, first_in, second_in):
    vmem = pl.BlockSpec(memory_space=pltpu.VMEM)
    hbm = pl.BlockSpec(memory_space=pltpu.HBM)
    bf16, f32 = jnp.bfloat16, jnp.float32
    outs = (
        jax.ShapeDtypeStruct((224, 512), bf16),
        jax.ShapeDtypeStruct((64, 224), f32),
        jax.ShapeDtypeStruct((64, 224), f32),
    )
    results = pl.pallas_call(
        main_kernel,
        out_shape=outs,
        in_specs=[hbm] * 5,
        out_specs=(vmem, hbm, hbm),
        scratch_shapes=[
            pltpu.VMEM((2, 128, 4096), bf16),
            pltpu.VMEM((224, 8192), bf16),
            pltpu.VMEM((64, 512), bf16),
            pltpu.VMEM((64, 224), f32),
            pltpu.VMEM((64, 224), f32),
            pltpu.VMEM((PARTS, 4, 4, 4, 64, 128), bf16),
            pltpu.VMEM((PARTS, 4, 4, 4, 128, 128), bf16),
            pltpu.VMEM((2, 128, 128), bf16),
            pltpu.VMEM((2, 64, 224), f32),
            pltpu.VMEM((PARTS, 128, 512), bf16),
            pltpu.VMEM((PARTS, 256, 128), f32),
            pltpu.VMEM((2, 256, 128), f32),
            pltpu.VMEM((2, 2, 64, 256), f32),
            pltpu.VMEM((2, 2, 64, 256), bf16),
            pltpu.VMEM((3, 64, 256), bf16),
            pltpu.VMEM((8, 64, 256), bf16),
            pltpu.SemaphoreType.DMA((SENDS,)),
            pltpu.SemaphoreType.DMA((RECEIVES,)),
            pltpu.SemaphoreType.DMA((7,)),
            pltpu.SemaphoreType.REGULAR((2,)),
        ],
        compiler_params=pltpu.CompilerParams(
            collective_id=0, has_side_effects=True, vmem_limit_bytes=66_600_000
        ),
        name="gather_reduce",
    )(tokens, grad_out, basis, first_in.T, second_in.T)
    update, first, second = pl.pallas_call(
        last_kernel,
        out_shape=outs,
        in_specs=[hbm] * 3,
        out_specs=(hbm,) * 3,
        scratch_shapes=[pltpu.VMEM(o.shape, o.dtype) for o in outs] + [pltpu.SemaphoreType.DMA((6,))],
        compiler_params=pltpu.CompilerParams(vmem_limit_bytes=66_600_000),
        name="results",
    )(*results)
    return update, first.T, second.T


def solution(mesh):
    in_specs = (P(("dp", "mp"), None), P("mp", "dp"), P("mp", None), P("mp", "dp"), P("mp", "dp"))
    out_specs = (P("mp", "dp"), P("mp", "dp"), P("mp", "dp"))
    return jax.shard_map(
        per_device, mesh=mesh, in_specs=in_specs, out_specs=out_specs, check_vma=False
    )
```
